256 devices in a mesh: lat: 64 (over x, z, core), wid: 4 (over y).
Axes of the slice: x: 4, y: 4, z: 8, core: 2. Of those that a mesh axis runs over, the one named last changes fastest.
Arguments:
- tokens: bfloat16 [1024, 8192], P('lat', 'wid'), may hold values from -1 to 1
- latent_rows: int32 [1024, 32], P('lat'), may hold values from 0 to 12287, as said below
- dec_bias: bfloat16 [8192], P('wid'), may hold values from -1.5 to 1.5
- enc_rows: bfloat16 [12288, 8192], P('lat', 'wid'), may hold values from -0.25 to 0.25
- latent_encoder_bias: float32 [12288], P('lat'), may hold values from -3 to 3
- dec_rows: bfloat16 [12288, 8192], P('lat', 'wid'), may hold values from -1 to 1
- enc_m: bfloat16 [12288, 8192], P('lat', 'wid'), may hold values from -12 to 12
- enc_v: bfloat16 [12288, 8192], P('lat', 'wid'), may hold values from 1 to 64
- dec_m: bfloat16 [12288, 8192], P('lat', 'wid'), may hold values from -6 to 6
- dec_v: bfloat16 [12288, 8192], P('lat', 'wid'), may hold values from 0.5 to 8
Outputs:
- enc_step: float32 [12288, 8192], P('lat', 'wid')
- dec_step: float32 [12288, 8192], P('lat', 'wid')
- enc_m_new: bfloat16 [12288, 8192], P('lat', 'wid')
- enc_v_new: bfloat16 [12288, 8192], P('lat', 'wid')
- dec_m_new: bfloat16 [12288, 8192], P('lat', 'wid')
- dec_v_new: bfloat16 [12288, 8192], P('lat', 'wid')
The draws below stay inside these ranges and needn't reach their ends.
Inputs may be any that keep to these rules, and one draw needn't show every extreme that they name: `latent_rows`: row r is held by index r // 192 of lat. Each token's 32 rows are distinct. The pairs of the 16 tokens of one index of lat name the rows of any one index of lat at most 24 times, and exactly 24 times for some index of lat in every such block.
All inputs are finite; a program needn't handle non-finite values.
Results may differ from the reference program's by a relative error of at most 0.0045.
Values may be sent and summed in bfloat16 or wider, within the bound.
No kernel may reach another device: no remote copies, remote signals or barrier semaphores. Data moves between devices by JAX's collectives and lax.ppermute only.
A program may use at most 128 MiB of HBM per device.

```python
import math
import jax
import jax.numpy as jnp
from jax import lax

D = 8192
K = 32
TOK_DEV = 16
R_DEV = 192
TOKENS = 1024
ROWS = 12288


def draw_latent_rows(key, part):
    key = jax.random.fold_in(key, 7)
    owners = TOKENS // TOK_DEV
    pairs = TOK_DEV * K
    half = pairs // owners // 2
    group = jnp.array([6, 2, 2, 2, 1, 1, 1, 1], jnp.int32) * half
    base = jnp.tile(group, owners // 8)
    keys = jax.random.split(key, owners)

    def one_block(block_key):
        perm_key, offset_key, shuffle_key = jax.random.split(block_key, 3)
        counts = base[jax.random.permutation(perm_key, owners)]
        owner_list = jnp.repeat(jnp.arange(owners, dtype=jnp.int32), counts, total_repeat_length=pairs)
        starts = jnp.cumsum(counts) - counts
        rank = jnp.arange(pairs, dtype=jnp.int32) - starts[owner_list]
        offsets = jax.random.randint(offset_key, (owners,), 0, R_DEV, dtype=jnp.int32)
        slot = (offsets[owner_list] + rank) % R_DEV
        chosen = owner_list * R_DEV + slot
        chosen = chosen[jax.random.permutation(shuffle_key, pairs)]
        return chosen.reshape(TOK_DEV, K)
    return jax.vmap(one_block)(keys).reshape(TOKENS, K).astype(jnp.int32)


def levels(stream_key, extent, pieces, low, top_value):
    loudness = 1.0
    for dim, shards_of in pieces:
        draws = jax.random.uniform(jax.random.fold_in(jax.random.fold_in(stream_key, 6), dim), (shards_of,), jnp.float32, low / len(pieces), top_value / len(pieces))
        loudness = loudness * jnp.repeat(jnp.exp(draws), extent[dim] // shards_of).reshape((-1,) + (1,) * (len(extent) - 1 - dim))
    return loudness


def bell_draw(rng, dims, deviation, most, pieces=(), kind=jnp.bfloat16):
    factor_of = levels(rng, dims, pieces, -0.22, 0.18) if pieces else 1.0
    values = jax.random.normal(rng, dims, jnp.float32) * deviation * factor_of
    return jnp.minimum(jnp.maximum(values, -most), most).astype(kind)


def setup_inputs(seed: int = 0) -> dict:
    streams_of = jax.random.split(jax.random.key(seed), 11)
    tokens = bell_draw(streams_of[0], (TOKENS, D), 0.125, 1.0, ((0, 64), (1, 4)))
    latent_rows = draw_latent_rows(jax.random.fold_in(streams_of[10], 71), 0)
    dec_bias = bell_draw(streams_of[2], (D,), 0.25, 1.5, ((0, 4),))
    enc_rows = bell_draw(streams_of[3], (ROWS, D), 512 ** -0.5, 0.25, ((0, 64), (1, 4)))
    latent_encoder_bias = bell_draw(streams_of[4], (ROWS,), 0.5, 3.0, ((0, 64),), jnp.float32)
    dec_rows = bell_draw(streams_of[5], (ROWS, D), K ** -0.5, 1.0, ((0, 64), (1, 4)))
    enc_m = bell_draw(streams_of[6], (ROWS, D), 2.0, 12.0, ((0, 64), (1, 4)))
    enc_v = jnp.clip(jnp.exp(math.log(64.0) - 4.158883 * jax.random.uniform(streams_of[7], (ROWS, D), jnp.float32) ** levels(streams_of[7], (ROWS, D), ((0, 64), (1, 4)), -0.2, 0.2)), 1.0, 64.0).astype(jnp.bfloat16)
    dec_m = bell_draw(streams_of[8], (ROWS, D), 1.0, 6.0, ((0, 64), (1, 4)))
    dec_v = jnp.clip(jnp.exp(math.log(8.0) - 2.7725887 * jax.random.uniform(streams_of[9], (ROWS, D), jnp.float32) ** levels(streams_of[9], (ROWS, D), ((0, 64), (1, 4)), -0.2, 0.2)), 0.5, 8.0).astype(jnp.bfloat16)
    return dict(tokens=tokens, latent_rows=latent_rows, dec_bias=dec_bias, enc_rows=enc_rows, latent_encoder_bias=latent_encoder_bias, dec_rows=dec_rows, enc_m=enc_m, enc_v=enc_v, dec_m=dec_m, dec_v=dec_v)


def rounded(value):
    return lax.optimization_barrier(value.astype(jnp.bfloat16)).astype(jnp.float32)

def adam_rows(grad, moment, second):
    first_new = 0.9 * moment.astype(jnp.float32) + 0.1 * grad
    second_new = 0.95 * second.astype(jnp.float32) + 0.05 * grad * grad
    step = first_new / (1.0 - 0.9 ** 10) / (jnp.sqrt(second_new / (1.0 - 0.95 ** 10)) + 1e-08)
    return (step, first_new.astype(jnp.bfloat16), second_new.astype(jnp.bfloat16))

def reference(tokens, latent_rows, dec_bias, enc_rows, latent_encoder_bias, dec_rows, enc_m, enc_v, dec_m, dec_v):
    bias_full = dec_bias.astype(jnp.float32)

    def one_block(carry, inputs):
        enc_acc, dec_acc = carry
        block_tokens, row_group_block = inputs
        input_centered = rounded(block_tokens.astype(jnp.float32) - bias_full)
        selected_encoder_weight = enc_rows[row_group_block].astype(jnp.float32)
        selected_decoder_weight = dec_rows[row_group_block].astype(jnp.float32)
        preactivation = jnp.einsum('znp,zp->zn', selected_encoder_weight, input_centered) + latent_encoder_bias[row_group_block]
        contrib = rounded(preactivation[:, :, None] * selected_decoder_weight)
        recon = bias_full + lax.optimization_barrier(jnp.sum(contrib, axis=1))
        residual_error = rounded(recon - block_tokens.astype(jnp.float32))
        gradient_inner = jnp.einsum('znp,zp->zn', selected_decoder_weight, residual_error)
        dec_term = rounded(preactivation[:, :, None] * residual_error[:, None, :])
        enc_term = rounded(gradient_inner[:, :, None] * input_centered[:, None, :])
        flat = row_group_block.reshape(-1)
        enc_acc = enc_acc.at[flat].add(enc_term.reshape(-1, D))
        dec_acc = dec_acc.at[flat].add(dec_term.reshape(-1, D))
        return ((enc_acc, dec_acc), None)
    blocks = TOKENS // TOK_DEV
    zeros = jnp.zeros((ROWS, D), jnp.float32)
    (enc_grad, dec_grad), unused = lax.scan(one_block, (zeros, zeros), (tokens.reshape(blocks, TOK_DEV, D), latent_rows.reshape(blocks, TOK_DEV, K)))
    enc_step, enc_m_new, enc_v_new = adam_rows(enc_grad, enc_m, enc_v)
    dec_step, dec_m_new, dec_v_new = adam_rows(dec_grad, dec_m, dec_v)
    return (enc_step, dec_step, enc_m_new, enc_v_new, dec_m_new, dec_v_new)
```

```python
import functools

import jax
import jax.numpy as jnp
from jax import lax
from jax.experimental import pallas as pl
from jax.experimental.pallas import tpu as pltpu
from jax.sharding import PartitionSpec as P

F32 = jnp.float32
BF16 = jnp.bfloat16
NX, NZ = 4, 8
CAP = 24
VMEM_LIMIT = 40 * 1024 * 1024


def plane_shift(value, dx, dz):
    pairs = []
    for i in range(2 * NX * NZ):
        x, z, core = i // (2 * NZ), (i // 2) % NZ, i % 2
        pairs.append((i, (((x + dx) % NX) * NZ + (z + dz) % NZ) * 2 + core))
    return lax.ppermute(value, "lat", pairs)


def core_swap(value):
    return lax.ppermute(value, "lat", [(i, i ^ 1) for i in range(2 * NX * NZ)])


def plane_gather(unit):
    near = [unit] + [plane_shift(unit, dx, 0) for dx in (1, -1, 2)]
    home = jnp.concatenate(near, axis=0)
    groups = [home]
    up = down = home
    for step in range(4):
        up = plane_shift(up, 0, 1)
        groups.append(up)
        if step < 3:
            down = plane_shift(down, 0, -1)
            groups.append(down)
    return groups


def dot(a, b, dims):
    return lax.dot_general(a, b, (dims, ((), ())), preferred_element_type=F32)


def two(value):
    high = value.astype(BF16)
    return high, (value - high.astype(F32)).astype(BF16)


def pick(dense, spread, rows_hot):
    high, low = two(dense)
    by_slot = dot(high, rows_hot, ((1,), (1,))) + dot(low, rows_hot, ((1,), (1,)))
    return jnp.sum(by_slot * spread.astype(F32), axis=0, keepdims=True)


def put(values, spread, rows_hot):
    high, low = two(spread.astype(F32) * values)
    return dot(high, rows_hot, ((1,), (0,))) + dot(low, rows_hot, ((1,), (0,)))


def encode_kernel(ids, x_ref, own_ref, other_ref, bias_ref, val_ref, spread_ref, hot_ref):
    tokens = x_ref.shape[0]
    row_count, width = own_ref.shape
    slots = spread_ref.shape[2]
    block = tokens * CAP // slots
    info = x_ref[:, width : width + 128].astype(F32)
    loc_one = pltpu.roll(info, 96, axis=1) + 1.0
    lane = lax.broadcasted_iota(jnp.int32, (tokens, 128), 1)
    before = (
        lax.broadcasted_iota(jnp.int32, (128, 128), 0)
        < lax.broadcasted_iota(jnp.int32, (128, 128), 1)
    ).astype(F32).astype(BF16)
    t_row = lax.broadcasted_iota(jnp.int32, (tokens, tokens), 0)
    t_col = lax.broadcasted_iota(jnp.int32, (tokens, tokens), 1)
    earlier = ((t_col < t_row) & (t_col // block == t_row // block)).astype(F32).astype(BF16)
    ones = jnp.ones((128, slots), BF16)
    base = (lax.broadcasted_iota(jnp.int32, (tokens, slots), 0) // block * CAP).astype(F32)
    slot_lane = lax.broadcasted_iota(jnp.int32, (tokens, slots), 1).astype(F32)
    slot_one = lax.broadcasted_iota(jnp.int32, (slots, 128), 0).astype(F32) + 1.0
    row_one = lax.broadcasted_iota(jnp.int32, (slots, row_count), 1).astype(F32) + 1.0
    for o in range(2):
        owned = (info == ids[o].astype(F32)) & (lane < 32)
        owned_b = owned.astype(F32).astype(BF16)
        in_token = dot(owned_b, before, ((1,), (0,)))
        count = dot(owned_b, ones, ((1,), (0,)))
        start = base + dot(earlier, count.astype(BF16), ((1,), (0,)))
        spread = ((slot_lane >= start) & (slot_lane < start + count)).astype(F32).astype(BF16)
        number = jnp.where(owned, start[:, :128] + in_token + 1.0, 0.0).astype(BF16)
        place = jnp.where(owned, loc_one, 0.0).astype(BF16)
        slot_number = dot(spread, number, ((0,), (0,)))
        slot_place = dot(spread, place, ((0,), (0,)))
        row = jnp.sum(jnp.where(slot_number == slot_one, slot_place, 0.0), axis=1, keepdims=True)
        hot = (row == row_one).astype(F32).astype(BF16)
        rows = own_ref if o == 0 else other_ref
        dense = dot(x_ref[:, :width], rows[...], ((1,), (1,)))
        if o == 0:
            dense = dense + bias_ref[...] * ids[2].astype(F32)
        val_ref[o] = pick(dense, spread, hot)
        spread_ref[o] = spread
        hot_ref[o] = hot


def recon_kernel(arrivals, split, *refs):
    val_ref, spread_ref, hot_ref, own_ref, other_ref = refs[:5]
    come = refs[5 : 5 + arrivals]
    weight_ref, *outs = refs[5 + arrivals :]
    total = None
    for o in range(2):
        weight = put(val_ref[o], spread_ref[o], hot_ref[o])
        high, low = two(weight)
        weight_ref[o, 0] = high
        weight_ref[o, 1] = low
        rows = (own_ref if o == 0 else other_ref)[...]
        term = dot(high, rows, ((1,), (0,))) + dot(low, rows, ((1,), (0,)))
        total = term if total is None else total + term
    for c in come:
        total = total + c[...].astype(F32)
    if split:
        unit = total.shape[0] // NX
        for k, out in enumerate(outs):
            out[...] = total[k * unit : (k + 1) * unit].astype(out.dtype)
    else:
        outs[0][...] = total.astype(BF16)


def inner_kernel(err_ref, spread_ref, hot_ref, own_ref, other_ref, val_ref):
    for o in range(2):
        rows = own_ref if o == 0 else other_ref
        val_ref[o] = pick(dot(err_ref[...], rows[...], ((1,), (1,))), spread_ref[o], hot_ref[o])


def dec_grad_kernel(n, *refs):
    errs, weights = refs[:n], refs[n : 2 * n]
    outs = refs[2 * n :]
    for o in range(2):
        total = None
        for err, weight in zip(errs, weights):
            e = err[...]
            term = dot(weight[o, 0], e, ((0,), (0,))) + dot(weight[o, 1], e, ((0,), (0,)))
            total = term if total is None else total + term
        outs[o][...] = total


def enc_grad_kernel(n, val_ref, *refs):
    xs, spreads, hots = refs[:n], refs[n : 2 * n], refs[2 * n : 3 * n]
    outs = refs[3 * n :]
    width = outs[0].shape[1]
    for o in range(2):
        total = None
        for g in range(n):
            weight = put(val_ref[o, g : g + 1], spreads[g][o], hots[g][o])
            high, low = two(weight)
            x = xs[g][:, :width]
            term = dot(high, x, ((0,), (0,))) + dot(low, x, ((0,), (0,)))
            total = term if total is None else total + term
        outs[o][...] = total


def adam_kernel(ids, own_ref, come_ref, m_ref, v_ref, step_ref, m_out, v_out):
    mine = pl.program_id(1) == ids[0]
    grad = jnp.where(mine, own_ref[...], come_ref[...])
    first = 0.9 * m_ref[...].astype(F32) + 0.1 * grad
    second = 0.95 * v_ref[...].astype(F32) + 0.05 * grad * grad
    step_ref[...] = (
        first / (1.0 - 0.9**10) / (jnp.sqrt(second / (1.0 - 0.95**10)) + 1e-08)
    )
    m_out[...] = first.astype(BF16)
    v_out[...] = second.astype(BF16)


def whole(kernel, outs, args, scalars=None, flops=0):
    vm = pl.BlockSpec(memory_space=pltpu.VMEM)
    sm = pl.BlockSpec(memory_space=pltpu.SMEM)
    specs = ([sm] if scalars is not None else []) + [vm] * len(args)
    size = sum(a.size * a.dtype.itemsize for a in args) + sum(
        o.size * o.dtype.itemsize for o in outs
    )
    call = pl.pallas_call(
        kernel,
        out_shape=tuple(outs),
        in_specs=specs,
        out_specs=(vm,) * len(outs),
        compiler_params=pltpu.CompilerParams(vmem_limit_bytes=VMEM_LIMIT),
        cost_estimate=pl.CostEstimate(flops=flops, bytes_accessed=size, transcendentals=0),
    )
    return call(*(([scalars] if scalars is not None else []) + list(args)))


def shape(*dims, kind=F32):
    return jax.ShapeDtypeStruct(dims, kind)


def wid_core_sum(values):
    values = values + core_swap(values)[::-1]
    n = lax.axis_size("wid")
    parts = [values]
    for k in range(1, n):
        parts.append(lax.ppermute(values, "wid", [(i, (i + k) % n) for i in range(n)]))
    return functools.reduce(jnp.add, parts)


def adam(core, own, come, moment, second):
    rows, full = moment.shape
    half = full // 2
    tile = rows // 4
    half_spec = pl.BlockSpec((tile, half), lambda i, h, ids: (i, 0))
    full_spec = pl.BlockSpec((tile, half), lambda i, h, ids: (i, h))
    return pl.pallas_call(
        adam_kernel,
        out_shape=(shape(rows, full), shape(rows, full, kind=BF16), shape(rows, full, kind=BF16)),
        grid_spec=pltpu.PrefetchScalarGridSpec(
            num_scalar_prefetch=1,
            grid=(rows // tile, 2),
            in_specs=[half_spec, half_spec, full_spec, full_spec],
            out_specs=(full_spec, full_spec, full_spec),
        ),
        compiler_params=pltpu.CompilerParams(vmem_limit_bytes=VMEM_LIMIT),
        cost_estimate=pl.CostEstimate(
            flops=rows * full * 12, bytes_accessed=rows * full * 16, transcendentals=0
        ),
    )(core.reshape(1), own, come, moment, second)


def local(tokens, latent_rows, dec_bias, enc_rows, latent_encoder_bias, dec_rows, enc_m, enc_v, dec_m, dec_v):
    me = lax.axis_index("lat")
    core = me % 2
    tok_dev, full = tokens.shape
    row_count = enc_rows.shape[0]
    half = full // 2
    mine, other = core * half, (1 - core) * half
    first_wid = (lax.axis_index("wid") == 0).astype(jnp.int32)
    ids = jnp.stack([me, me ^ 1, first_wid]).astype(jnp.int32)

    info = jnp.concatenate(
        [
            (latent_rows // row_count).astype(BF16),
            (latent_rows % row_count).astype(BF16),
            jnp.zeros((tok_dev, 128 - 2 * latent_rows.shape[1]), BF16),
        ],
        axis=1,
    )
    cut = lambda a, at: lax.dynamic_slice_in_dim(a, at, half, axis=a.ndim - 1)
    own_part = jnp.concatenate([cut(tokens, mine), info], axis=1)
    come_part = core_swap(jnp.concatenate([cut(tokens, other), info], axis=1))
    even = core == 0
    unit_raw = jnp.concatenate(
        [jnp.where(even, own_part, come_part), jnp.where(even, come_part, own_part)], axis=0
    )
    bias_half = cut(dec_bias, mine).astype(F32)
    raw = unit_raw[:, :half].astype(F32)
    unit = jnp.concatenate([(raw - bias_half).astype(BF16), unit_raw[:, half:]], axis=1)
    come_rows = core_swap(jnp.stack([cut(enc_rows, other), cut(dec_rows, other)]))
    enc_own, dec_own = cut(enc_rows, mine), cut(dec_rows, mine)
    enc_other, dec_other = come_rows[0], come_rows[1]
    row_bias = latent_encoder_bias.reshape(1, row_count)

    xs = plane_gather(unit)
    groups = len(xs)
    group_tok = xs[0].shape[0]
    slots = group_tok // tok_dev * CAP
    flops = 2 * group_tok * 2 * row_count * half
    vals, spreads, hots = [], [], []
    for x in xs:
        v, s, h = whole(
            encode_kernel,
            [
                shape(2, 1, slots),
                shape(2, group_tok, slots, kind=BF16),
                shape(2, slots, row_count, kind=BF16),
            ],
            [x, enc_own, enc_other, row_bias],
            scalars=ids,
            flops=flops,
        )
        vals.append(v)
        spreads.append(s)
        hots.append(h)
    pre = wid_core_sum(jnp.concatenate(vals, axis=1))

    weights = [None] * groups

    def recon(g, come, split=False):
        unit_tok = group_tok // NX
        outs = (
            [shape(unit_tok, half)] + [shape(unit_tok, half, kind=BF16)] * (NX - 1)
            if split
            else [shape(group_tok, half, kind=BF16)]
        )
        weights[g], *rest = whole(
            functools.partial(recon_kernel, len(come), split),
            [shape(2, 2, group_tok, row_count, kind=BF16)] + outs,
            [pre[:, g : g + 1], spreads[g], hots[g], dec_own, dec_other] + come,
            flops=2 * flops,
        )
        return rest

    up = recon(7, [])[0]
    down = recon(6, [])[0]
    for g_up, g_down in ((5, 4), (3, 2)):
        up = recon(g_up, [plane_shift(up, 0, -1)])[0]
        down = recon(g_down, [plane_shift(down, 0, 1)])[0]
    up = recon(1, [plane_shift(up, 0, -1)])[0]
    home, *away = recon(0, [plane_shift(up, 0, -1), plane_shift(down, 0, 1)], split=True)
    total = home
    for dx, part in zip((-1, 1, -2), away):
        total = total + plane_shift(part, dx, 0).astype(F32)
    err = (total + bias_half - raw).astype(BF16)

    errs = plane_gather(err)
    dots = [
        whole(
            inner_kernel,
            [shape(2, 1, slots)],
            [e, s, h, dec_own, dec_other],
            flops=flops,
        )[0]
        for e, s, h in zip(errs, spreads, hots)
    ]
    dz = wid_core_sum(jnp.concatenate(dots, axis=1))
    grad_shapes = [shape(row_count, half)] * 2
    dec_mine, dec_away = whole(
        functools.partial(dec_grad_kernel, groups), grad_shapes, errs + weights, flops=16 * flops
    )
    dec_step, dec_m_new, dec_v_new = adam(core, dec_mine, core_swap(dec_away), dec_m, dec_v)
    enc_mine, enc_away = whole(
        functools.partial(enc_grad_kernel, groups),
        grad_shapes,
        [dz] + xs + spreads + hots,
        flops=16 * flops,
    )
    enc_step, enc_m_new, enc_v_new = adam(core, enc_mine, core_swap(enc_away), enc_m, enc_v)
    return (enc_step, dec_step, enc_m_new, enc_v_new, dec_m_new, dec_v_new)


def solution(mesh):
    grid = P("lat", "wid")
    return jax.shard_map(
        local,
        mesh=mesh,
        in_specs=(grid, P("lat", None), P("wid"), grid, P("lat"), grid, grid, grid, grid, grid),
        out_specs=(grid,) * 6,
        check_vma=False,
    )
```

```python
import functools

import jax
import jax.numpy as jnp
from jax import lax
from jax.experimental import pallas as pl
from jax.experimental.pallas import tpu as pltpu
from jax.sharding import PartitionSpec as P

F32 = jnp.float32
BF16 = jnp.bfloat16
NX, NZ = 4, 8
CAP = 24
VMEM_LIMIT = 12 * 1024 * 1024
FROM = {1: (1, 3, 0, 2), -1: (2, 0, 3, 1), 2: (3, 2, 1, 0)}


def plane_shift(value, dx, dz):
    pairs = []
    for i in range(2 * NX * NZ):
        x, z, core = i // (2 * NZ), (i // 2) % NZ, i % 2
        pairs.append((i, (((x + dx) % NX) * NZ + (z + dz) % NZ) * 2 + core))
    return lax.ppermute(value, "lat", pairs)


def core_swap(value):
    return lax.ppermute(value, "lat", [(i, i ^ 1) for i in range(2 * NX * NZ)])


def tie(first, *rest):
    return lax.optimization_barrier((first, *rest))[0]


def z_gather(home, work):
    up = down = home
    done = [[work(0, home)]]
    out = {0: done[0][0]}
    for step in range(4):
        if step >= 1:
            up = tie(up, *jax.tree.leaves(done[step - 1]))
        up = plane_shift(up, 0, 1)
        now = [(2 * step + 1, up)]
        if step < 3:
            down = plane_shift(down, 0, -1)
            now.append((2 * step + 2, down))
        done.append([])
        for g, value in now:
            out[g] = work(g, value)
            done[-1].append(out[g])
    return [out[g] for g in range(NZ)]


def dot(a, b, dims):
    return lax.dot_general(a, b, (dims, ((), ())), preferred_element_type=F32)


def pick(dense, spread, rows_hot):
    high = dense.astype(BF16)
    low = (dense - high.astype(F32)).astype(BF16)
    by_slot = dot(high, rows_hot, ((1,), (1,))) + dot(low, rows_hot, ((1,), (1,)))
    return jnp.sum(by_slot * spread.astype(F32), axis=0, keepdims=True)


def flag(mask):
    return mask.astype(F32).astype(BF16)


def encode_kernel(ids, x_ref, bias_ref, own_ref, other_ref, row_bias_ref, val_ref, spread_ref, hot_ref, slot_ref):
    tokens = x_ref.shape[0]
    row_count, width = own_ref.shape
    slots = spread_ref.shape[2]
    block = tokens * CAP // slots
    info = x_ref[:, width : width + 128].astype(F32)
    loc_one = pltpu.roll(info, 96, axis=1) + 1.0
    iota = lambda dims, axis: lax.broadcasted_iota(jnp.int32, dims, axis)
    lane = iota((tokens, 128), 1)
    before = flag(iota((128, 128), 0) < iota((128, 128), 1))
    t_row, t_col = iota((tokens, tokens), 0), iota((tokens, tokens), 1)
    earlier = flag((t_col < t_row) & (t_col // block == t_row // block))
    ones = jnp.ones((128, slots), BF16)
    base = (iota((tokens, slots), 0) // block * CAP).astype(F32)
    slot_lane = iota((tokens, slots), 1).astype(F32)
    slot_one = iota((slots, 128), 0).astype(F32) + 1.0
    row_one = iota((slots, row_count), 1).astype(F32) + 1.0
    x = (x_ref[:, :width].astype(F32) - bias_ref[...].astype(F32)).astype(BF16)
    two = range(2)
    owned = [(info == ids[o].astype(F32)) & (lane < 32) for o in two]
    owned_b = [flag(w) for w in owned]
    dense = [dot(x, r[...], ((1,), (1,))) for r in (own_ref, other_ref)]
    in_token = [dot(w, before, ((1,), (0,))) for w in owned_b]
    count = [dot(w, ones, ((1,), (0,))) for w in owned_b]
    start = [base + dot(earlier, c.astype(BF16), ((1,), (0,))) for c in count]
    spread = [flag((slot_lane >= start[o]) & (slot_lane < start[o] + count[o])) for o in two]
    number = [jnp.where(owned[o], start[o][:, :128] + in_token[o] + 1.0, 0.0).astype(BF16) for o in two]
    place = [jnp.where(w, loc_one, 0.0).astype(BF16) for w in owned]
    slot_number = [dot(spread[o], number[o], ((0,), (0,))) for o in two]
    slot_place = [dot(spread[o], place[o], ((0,), (0,))) for o in two]
    row = [
        jnp.sum(jnp.where(slot_number[o] == slot_one, slot_place[o], 0.0), axis=1, keepdims=True)
        for o in two
    ]
    hot = [flag(row[o] == row_one) for o in two]
    dense[0] = dense[0] + row_bias_ref[...] * ids[2].astype(F32)
    for o in two:
        val_ref[o] = pick(dense[o], spread[o], hot[o])
        spread_ref[o] = spread[o]
        hot_ref[o] = hot[o]
        slot_ref[o] = dot(spread[o], x, ((0,), (0,))).astype(BF16)


def column(values):
    return jnp.transpose(jnp.broadcast_to(values, (8, values.shape[1])))[:, :1]


def recon_kernel(arrivals, *refs):
    val_ref, spread_ref, hot_ref, own_ref, other_ref = refs[:5]
    come = refs[5 : 5 + arrivals]
    outs = refs[5 + arrivals :]
    total = None
    for o in range(2):
        rows = dot(hot_ref[o], (own_ref if o == 0 else other_ref)[...], ((1,), (0,)))
        contrib = (column(val_ref[o]) * rows).astype(BF16)
        term = dot(spread_ref[o], contrib, ((1,), (0,)))
        total = term if total is None else total + term
    for c in come:
        total = total + c[...].astype(F32)
    for out in outs:
        out[...] = total.astype(out.dtype)


def err_kernel(unit, sum_ref, up_ref, down_ref, far_up_ref, far_down_ref, x_ref, bias_ref, err_ref):
    width = err_ref.shape[1]
    piece = lambda ref, k: ref[k * unit : (k + 1) * unit, :].astype(F32)
    for k in range(NX):
        total = piece(sum_ref, k)
        total = total + piece(up_ref, FROM[1].index(k))
        total = total + piece(down_ref, FROM[-1].index(k))
        far = FROM[2].index(k)
        total = total + (piece(far_up_ref, far) if far < 2 else piece(far_down_ref, far - 2))
        recon = bias_ref[...].astype(F32) + total
        raw = x_ref[k * unit : (k + 1) * unit, :width].astype(F32)
        err_ref[k * unit : (k + 1) * unit, :] = (recon - raw).astype(BF16)


def inner_kernel(first, err_ref, pre_ref, spread_ref, hot_ref, own_ref, other_ref, *refs):
    held, outs = (None, refs) if first else (refs[:2], refs[2:])
    val_ref, *grads = outs
    err = err_ref[...]
    for o in range(2):
        rows = own_ref if o == 0 else other_ref
        val_ref[o] = pick(dot(err, rows[...], ((1,), (1,))), spread_ref[o], hot_ref[o])
        by_slot = dot(spread_ref[o], err, ((0,), (0,)))
        term = (column(pre_ref[o]) * by_slot).astype(BF16)
        grad = dot(hot_ref[o], term, ((0,), (0,)))
        grads[o][...] = grad if first else held[o][...] + grad


def enc_grad_kernel(n, o, val_ref, *refs):
    slot_refs, hots, out = refs[:n], refs[n : 2 * n], refs[2 * n]
    values = jnp.transpose(val_ref[o])
    total = None
    for g in range(n):
        term = (values[:, g : g + 1] * slot_refs[g][o].astype(F32)).astype(BF16)
        grad = dot(hots[g][o], term, ((0,), (0,)))
        total = grad if total is None else total + grad
    out[...] = total


def adam_kernel(ids, own_ref, come_ref, m_ref, v_ref, step_ref, m_out, v_out):
    mine = pl.program_id(1) == ids[0]
    grad = jnp.where(mine, own_ref[...], come_ref[...])
    first = 0.9 * m_ref[...].astype(F32) + 0.1 * grad
    second = 0.95 * v_ref[...].astype(F32) + 0.05 * grad * grad
    step_ref[...] = (
        first / (1.0 - 0.9**10) / (jnp.sqrt(second / (1.0 - 0.95**10)) + 1e-08)
    )
    m_out[...] = first.astype(BF16)
    v_out[...] = second.astype(BF16)


def whole(kernel, outs, args, scalars=None, flops=0, aliases=None):
    vm = pl.BlockSpec(memory_space=pltpu.VMEM)
    sm = pl.BlockSpec(memory_space=pltpu.SMEM)
    specs = ([sm] if scalars is not None else []) + [vm] * len(args)
    size = sum(a.size * a.dtype.itemsize for a in args) + sum(
        o.size * o.dtype.itemsize for o in outs
    )
    call = pl.pallas_call(
        kernel,
        out_shape=tuple(outs),
        in_specs=specs,
        out_specs=(vm,) * len(outs),
        input_output_aliases=aliases or {},
        compiler_params=pltpu.CompilerParams(vmem_limit_bytes=VMEM_LIMIT),
        cost_estimate=pl.CostEstimate(flops=flops, bytes_accessed=size, transcendentals=0),
    )
    return call(*(([scalars] if scalars is not None else []) + list(args)))


def shape(*dims, kind=F32):
    return jax.ShapeDtypeStruct(dims, kind)


def wid_core_sum(values):
    values = values + core_swap(values)[::-1]
    for pairs in ([(0, 1), (1, 0), (2, 3), (3, 2)], [(0, 3), (3, 0), (1, 2), (2, 1)]):
        values = values + lax.ppermute(values, "wid", pairs)
    return values


def adam(core, own, come, moment, second):
    rows, full = moment.shape
    half = full // 2
    tile = rows // 4
    half_spec = pl.BlockSpec((tile, half), lambda i, h, ids: (i, 0))
    full_spec = pl.BlockSpec((tile, half), lambda i, h, ids: (i, h))
    return pl.pallas_call(
        adam_kernel,
        out_shape=(shape(rows, full), shape(rows, full, kind=BF16), shape(rows, full, kind=BF16)),
        grid_spec=pltpu.PrefetchScalarGridSpec(
            num_scalar_prefetch=1,
            grid=(rows // tile, 2),
            in_specs=[half_spec, half_spec, full_spec, full_spec],
            out_specs=(full_spec, full_spec, full_spec),
        ),
        compiler_params=pltpu.CompilerParams(vmem_limit_bytes=VMEM_LIMIT),
        cost_estimate=pl.CostEstimate(
            flops=rows * full * 12, bytes_accessed=rows * full * 16, transcendentals=0
        ),
    )(core.reshape(1), own, come, moment, second)


def local(tokens, latent_rows, dec_bias, enc_rows, latent_encoder_bias, dec_rows, enc_m, enc_v, dec_m, dec_v):
    me = lax.axis_index("lat")
    core = me % 2
    tok_dev, full = tokens.shape
    row_count = enc_rows.shape[0]
    half = full // 2
    mine, other = core * half, (1 - core) * half
    first_wid = (lax.axis_index("wid") == 0).astype(jnp.int32)
    ids = jnp.stack([me, me ^ 1, first_wid]).astype(jnp.int32)

    info = jnp.concatenate(
        [
            (latent_rows // row_count).astype(BF16),
            (latent_rows % row_count).astype(BF16),
            jnp.zeros((tok_dev, 128 - 2 * latent_rows.shape[1]), BF16),
        ],
        axis=1,
    )
    cut = lambda a, at: lax.dynamic_slice_in_dim(a, at, half, axis=a.ndim - 1)
    own_part = jnp.concatenate([cut(tokens, mine), info], axis=1)
    come_part = core_swap(jnp.concatenate([cut(tokens, other), info], axis=1))
    even = core == 0
    unit = jnp.concatenate(
        [jnp.where(even, own_part, come_part), jnp.where(even, come_part, own_part)], axis=0
    )
    bias_half = cut(dec_bias, mine).reshape(1, half)
    row_bias = latent_encoder_bias.reshape(1, row_count)
    come_rows = core_swap(jnp.stack([cut(enc_rows, other), cut(dec_rows, other)]))
    enc_own, dec_own = cut(enc_rows, mine), cut(dec_rows, mine)
    home = jnp.concatenate([unit] + [plane_shift(unit, dx, 0) for dx in (1, -1, 2)], axis=0)
    home = tie(home, come_rows, enc_own, dec_own)
    enc_other, dec_other = come_rows[0], come_rows[1]

    group_tok = home.shape[0]
    unit_tok = group_tok // NX
    slots = group_tok // tok_dev * CAP
    flops = 2 * group_tok * 2 * row_count * half

    def encode(g, x):
        return whole(
            encode_kernel,
            [
                shape(2, 1, slots),
                shape(2, group_tok, slots, kind=BF16),
                shape(2, slots, row_count, kind=BF16),
                shape(2, slots, half, kind=BF16),
            ],
            [x, bias_half, enc_own, enc_other, row_bias],
            scalars=ids,
            flops=4 * flops,
        )

    vals, spreads, hots, xs = zip(*z_gather(home, encode))
    pre = wid_core_sum(jnp.concatenate(vals, axis=1))
    pres = [pre[:, g : g + 1] for g in range(NZ)]

    def recon(g, come, kinds=(BF16,)):
        return whole(
            functools.partial(recon_kernel, len(come)),
            [shape(group_tok, half, kind=k) for k in kinds],
            [pres[g], spreads[g], hots[g], dec_own, dec_other] + come,
            flops=2 * flops,
        )

    up = recon(7, [])[0]
    down = recon(6, [])[0]
    for g_up, g_down in ((5, 4), (3, 2)):
        up = recon(g_up, [plane_shift(up, 0, -1)])[0]
        down = recon(g_down, [plane_shift(down, 0, 1)])[0]
    up = recon(1, [plane_shift(up, 0, -1)])[0]
    exact, sent = recon(0, [plane_shift(up, 0, -1), plane_shift(down, 0, 1)], (F32, BF16))
    right, left = plane_shift(sent, 1, 0), plane_shift(sent, -1, 0)
    far_right = plane_shift(right[: 2 * unit_tok], 1, 0)
    far_left = plane_shift(left[2 * unit_tok :], -1, 0)
    (err_home,) = whole(
        functools.partial(err_kernel, unit_tok),
        [shape(group_tok, half, kind=BF16)],
        [exact, right, left, far_right, far_left, home, bias_half],
    )

    grads = []

    def inner(g, err):
        held = list(grads)
        value, *grads[:] = whole(
            functools.partial(inner_kernel, not held),
            [shape(2, 1, slots)] + [shape(row_count, half)] * 2,
            [err, pres[g], spreads[g], hots[g], dec_own, dec_other] + held,
            flops=4 * flops,
            aliases={6: 1, 7: 2} if held else None,
        )
        return value

    dz = wid_core_sum(jnp.concatenate(z_gather(err_home, inner), axis=1))
    dec_step, dec_m_new, dec_v_new = adam(core, grads[0], core_swap(grads[1]), dec_m, dec_v)
    enc_away, enc_mine = [
        whole(
            functools.partial(enc_grad_kernel, NZ, o),
            [shape(row_count, half)],
            [dz, *xs, *hots],
            flops=8 * flops,
        )[0]
        for o in (1, 0)
    ]
    enc_step, enc_m_new, enc_v_new = adam(core, enc_mine, core_swap(enc_away), enc_m, enc_v)
    return (enc_step, dec_step, enc_m_new, enc_v_new, dec_m_new, dec_v_new)


def solution(mesh):
    grid = P("lat", "wid")
    return jax.shard_map(
        local,
        mesh=mesh,
        in_specs=(grid, P("lat", None), P("wid"), grid, P("lat"), grid, grid, grid, grid, grid),
        out_specs=(grid,) * 6,
        check_vma=False,
    )
```

```python
import functools

import jax
import jax.numpy as jnp
from jax import lax
from jax.experimental import pallas as pl
from jax.experimental.pallas import tpu as pltpu
from jax.sharding import PartitionSpec as P

F32 = jnp.float32
BF16 = jnp.bfloat16
NX, NZ = 4, 8
CAP = 24
VMEM_LIMIT = 12 * 1024 * 1024
FROM = {1: (1, 3, 0, 2), -1: (2, 0, 3, 1), 2: (3, 2, 1, 0)}


def plane_shift(value, dx, dz):
    pairs = []
    for i in range(2 * NX * NZ):
        x, z, core = i // (2 * NZ), (i // 2) % NZ, i % 2
        pairs.append((i, (((x + dx) % NX) * NZ + (z + dz) % NZ) * 2 + core))
    return lax.ppermute(value, "lat", pairs)


def core_swap(value):
    return lax.ppermute(value, "lat", [(i, i ^ 1) for i in range(2 * NX * NZ)])


def tie(first, *rest):
    return lax.optimization_barrier((first, *rest))[0]


def z_gather(homes, work):
    up, down = list(homes), list(homes)
    out, done = [work([0], list(homes))], []
    for step in range(NZ // 2):
        if done:
            up[0] = tie(up[0], *done[-1])
        done.append(jax.tree.leaves(out[-1]))
        if step < NZ // 2 - 1:
            for h in range(2):
                up[h] = plane_shift(up[h], 0, 1)
                down[h] = plane_shift(down[h], 0, -1)
            out.append(work([2 * step + 1, 2 * step + 2], up + down))
        else:
            out.append(work([NZ - 1], [plane_shift(up[0], 0, 1), plane_shift(down[1], 0, -1)]))
    return out


def dot(a, b, dims):
    return lax.dot_general(a, b, (dims, ((), ())), preferred_element_type=F32)


def pick(dense, spread, rows_hot):
    high = dense.astype(BF16)
    low = (dense - high.astype(F32)).astype(BF16)
    by_slot = dot(high, rows_hot, ((1,), (1,))) + dot(low, rows_hot, ((1,), (1,)))
    return jnp.sum(by_slot * spread.astype(F32), axis=0, keepdims=True)


def flag(mask):
    return mask.astype(F32).astype(BF16)


def iota(dims, axis):
    return lax.broadcasted_iota(jnp.int32, dims, axis)


def hots(meta, o, tokens, row_count):
    slots = meta.shape[0] - tokens
    start = meta[:tokens, 2 * o : 2 * o + 1].astype(F32)
    end = meta[:tokens, 2 * o + 1 : 2 * o + 2].astype(F32)
    lane = iota((tokens, slots), 1).astype(F32)
    row = meta[tokens:, o : o + 1].astype(F32)
    row_one = iota((slots, row_count), 1).astype(F32) + 1.0
    return flag((lane >= start) & (lane < end)), flag(row == row_one)


def center(x, bias):
    return (x.astype(F32) - bias.astype(F32)).astype(BF16)


def encode_kernel(n, ids, *refs):
    xs, (bias_ref, own_ref, other_ref, row_bias_ref) = refs[: 2 * n], refs[2 * n : 2 * n + 4]
    val_ref, metas = refs[2 * n + 4], refs[2 * n + 5 :]
    tokens, part = xs[0].shape
    row_count, width = own_ref.shape
    slots = metas[0].shape[0] - tokens
    block = tokens * CAP // slots
    lane = iota((tokens, 128), 1)
    before = flag(iota((128, 128), 0) < iota((128, 128), 1))
    t_row, t_col = iota((tokens, tokens), 0), iota((tokens, tokens), 1)
    earlier = flag((t_col < t_row) & (t_col // block == t_row // block))
    ones = jnp.ones((128, slots), BF16)
    base = (iota((tokens, slots), 0) // block * CAP).astype(F32)
    slot_lane = iota((tokens, slots), 1).astype(F32)
    slot_one = iota((slots, 128), 0).astype(F32) + 1.0
    row_one = iota((slots, row_count), 1).astype(F32) + 1.0
    low_bias, high_bias = bias_ref[:, :part], bias_ref[:, part:]
    jobs = [(k, o) for k in range(n) for o in range(2)]
    infos = [xs[2 * k + 1][:, width - part :].astype(F32) for k in range(n)]
    loc_ones = [pltpu.roll(info, 96, axis=1) + 1.0 for info in infos]
    owned = [(infos[k] == ids[o].astype(F32)) & (lane < 32) for k, o in jobs]
    owned_b = [flag(w) for w in owned]
    count = [dot(w, ones, ((1,), (0,))) for w in owned_b]
    in_token = [dot(w, before, ((1,), (0,))) for w in owned_b]
    start = [base + dot(earlier, c.astype(BF16), ((1,), (0,))) for c in count]
    end = [s + c for s, c in zip(start, count)]
    spread = [flag((slot_lane >= s) & (slot_lane < e)) for s, e in zip(start, end)]
    number = [
        jnp.where(w, s[:, :128] + i + 1.0, 0.0).astype(BF16) for w, s, i in zip(owned, start, in_token)
    ]
    place = [jnp.where(w, loc_ones[k], 0.0).astype(BF16) for w, (k, o) in zip(owned, jobs)]
    slot_number = [dot(s, v, ((0,), (0,))) for s, v in zip(spread, number)]
    slot_place = [dot(s, v, ((0,), (0,))) for s, v in zip(spread, place)]
    row = [
        jnp.sum(jnp.where(v == slot_one, p, 0.0), axis=1, keepdims=True)
        for v, p in zip(slot_number, slot_place)
    ]
    lows = [center(xs[2 * k][...], low_bias) for k in range(n)]
    highs = [center(xs[2 * k + 1][:, : width - part], high_bias) for k in range(n)]
    for j, (k, o) in enumerate(jobs):
        rows = own_ref if o == 0 else other_ref
        dense = dot(lows[k], rows[:, :part], ((1,), (1,))) + dot(highs[k], rows[:, part:], ((1,), (1,)))
        if o == 0:
            dense = dense + row_bias_ref[...] * ids[2].astype(F32)
        val_ref[o, k : k + 1, :] = pick(dense, spread[j], flag(row[j] == row_one))
    slot_lane_128 = iota((slots, 128), 1)
    for k in range(n):
        s0, s1, e0, e1 = (v[2 * k + o][:, :128] for v in (start, end) for o in range(2))
        by_token = jnp.where(lane == 0, s0, jnp.where(lane == 1, e0, jnp.where(lane == 2, s1, e1)))
        metas[k][:tokens, :] = by_token.astype(BF16)
        metas[k][tokens:, :] = jnp.where(slot_lane_128 == 0, row[2 * k], row[2 * k + 1]).astype(BF16)


def column(values):
    return jnp.transpose(jnp.broadcast_to(values, (8, values.shape[1])))[:, :1]


def recon_kernel(arrivals, g, h, *refs):
    val_ref, meta_ref, own_ref, other_ref = refs[:4]
    come = refs[4 : 4 + arrivals]
    outs = refs[4 + arrivals :]
    tokens, part = outs[0].shape
    total = None
    for o in range(2):
        spread, hot = hots(meta_ref[...], o, tokens, own_ref.shape[0])
        weights = (own_ref if o == 0 else other_ref)[:, h * part : (h + 1) * part]
        rows = dot(hot, weights, ((1,), (0,)))
        contrib = (column(val_ref[o, g : g + 1, :]) * rows).astype(BF16)
        term = dot(spread, contrib, ((1,), (0,)))
        total = term if total is None else total + term
    for c in come:
        total = total + c[...].astype(F32)
    for out in outs:
        out[...] = total.astype(out.dtype)


def err_kernel(h, sum_ref, up_ref, down_ref, far_up_ref, far_down_ref, x_ref, bias_ref, err_ref):
    tokens, part = err_ref.shape
    unit = tokens // NX
    piece = lambda ref, k: ref[k * unit : (k + 1) * unit, :].astype(F32)
    for k in range(NX):
        total = piece(sum_ref, k)
        total = total + piece(up_ref, FROM[1].index(k))
        total = total + piece(down_ref, FROM[-1].index(k))
        far = FROM[2].index(k)
        total = total + (piece(far_up_ref, far) if far < 2 else piece(far_down_ref, far - 2))
        recon = bias_ref[:, h * part : (h + 1) * part].astype(F32) + total
        raw = x_ref[k * unit : (k + 1) * unit, :part].astype(F32)
        err_ref[k * unit : (k + 1) * unit, :] = (recon - raw).astype(BF16)


def inner_kernel(gs, first, *refs):
    n = len(gs)
    errs, metas, (pre_ref, own_ref, other_ref) = refs[: 2 * n], refs[2 * n : 3 * n], refs[3 * n : 3 * n + 3]
    held, outs = refs[3 * n + 3 : -3], refs[-3:]
    val_ref, *grads = outs
    tokens, part = errs[0].shape
    row_count = own_ref.shape[0]
    both = [[hots(m[...], o, tokens, row_count) for m in metas] for o in range(2)]
    for o in range(2):
        rows = own_ref if o == 0 else other_ref
        sums = [None, None]
        for k, g in enumerate(gs):
            spread, hot = both[o][k]
            dense = None
            pre = column(pre_ref[o, g : g + 1, :])
            for h in range(2):
                err = errs[2 * k + h][...]
                cols = slice(h * part, (h + 1) * part)
                d = dot(err, rows[:, cols], ((1,), (1,)))
                dense = d if dense is None else dense + d
                term = (pre * dot(spread, err, ((0,), (0,)))).astype(BF16)
                grad = dot(hot, term, ((0,), (0,)))
                sums[h] = grad if sums[h] is None else sums[h] + grad
            val_ref[o, k : k + 1, :] = pick(dense, spread, hot)
        for h in range(2):
            cols = slice(h * part, (h + 1) * part)
            grads[o][:, cols] = sums[h] if first else held[o][:, cols] + sums[h]


def enc_grad_kernel(n, val_ref, bias_ref, *refs):
    sources, outs = refs[: 3 * n], refs[3 * n : 3 * n + 2]
    buffers, sems = refs[3 * n + 2 : 3 * n + 5], refs[3 * n + 5]
    copies = []
    for g in range(n):
        for b in range(3):
            copies.append(
                pltpu.make_async_copy(sources[3 * g + b], buffers[b].at[g], sems.at[3 * g + b])
            )
    for copy in copies:
        copy.start()
    low, high, meta = buffers
    tokens, part = low.shape[1:]
    row_count, width = outs[0].shape
    values = [jnp.transpose(val_ref[o]) for o in range(2)]
    for g in range(n):
        for b in range(3):
            copies[3 * g + b].wait()
        x = [center(low[g], bias_ref[:, :part]), center(high[g, :, : width - part], bias_ref[:, part:])]
        for o in range(2):
            spread, hot = hots(meta[g], o, tokens, row_count)
            for h in range(2):
                cols = slice(h * part, (h + 1) * part)
                term = (values[o][:, g : g + 1] * dot(spread, x[h], ((0,), (0,)))).astype(BF16)
                grad = dot(hot, term, ((0,), (0,)))
                outs[o][:, cols] = grad if g == 0 else outs[o][:, cols] + grad


def adam_kernel(ids, own_ref, come_ref, m_ref, v_ref, step_ref, m_out, v_out):
    mine = pl.program_id(1) == ids[0]
    grad = jnp.where(mine, own_ref[...], come_ref[...])
    first = 0.9 * m_ref[...].astype(F32) + 0.1 * grad
    second = 0.95 * v_ref[...].astype(F32) + 0.05 * grad * grad
    scale = 1.0 / (1.0 - 0.9**10)
    step_ref[...] = first * scale / (jnp.sqrt(second * (1.0 / (1.0 - 0.95**10))) + 1e-08)
    m_out[...] = first.astype(BF16)
    v_out[...] = second.astype(BF16)


def whole(kernel, outs, args, scalars=None, flops=0, aliases=None):
    vm = pl.BlockSpec(memory_space=pltpu.VMEM)
    sm = pl.BlockSpec(memory_space=pltpu.SMEM)
    specs = ([sm] if scalars is not None else []) + [vm] * len(args)
    size = sum(a.size * a.dtype.itemsize for a in args) + sum(
        o.size * o.dtype.itemsize for o in outs
    )
    call = pl.pallas_call(
        kernel,
        out_shape=tuple(outs),
        in_specs=specs,
        out_specs=(vm,) * len(outs),
        input_output_aliases=aliases or {},
        compiler_params=pltpu.CompilerParams(vmem_limit_bytes=VMEM_LIMIT),
        cost_estimate=pl.CostEstimate(flops=flops, bytes_accessed=size, transcendentals=0),
    )
    return call(*(([scalars] if scalars is not None else []) + list(args)))


def shape(*dims, kind=F32):
    return jax.ShapeDtypeStruct(dims, kind)


def wid_core_sum(values):
    values = values + core_swap(values)[::-1]
    for pairs in ([(0, 1), (1, 0), (2, 3), (3, 2)], [(0, 3), (3, 0), (1, 2), (2, 1)]):
        values = values + lax.ppermute(values, "wid", pairs)
    return values


def adam(core, own, come, moment, second):
    rows, full = moment.shape
    half = full // 2
    tile = rows // 2
    half_spec = pl.BlockSpec((tile, half), lambda i, h, ids: (i, 0))
    full_spec = pl.BlockSpec((tile, half), lambda i, h, ids: (i, h))
    return pl.pallas_call(
        adam_kernel,
        out_shape=(shape(rows, full), shape(rows, full, kind=BF16), shape(rows, full, kind=BF16)),
        grid_spec=pltpu.PrefetchScalarGridSpec(
            num_scalar_prefetch=1,
            grid=(rows // tile, 2),
            in_specs=[half_spec, half_spec, full_spec, full_spec],
            out_specs=(full_spec, full_spec, full_spec),
        ),
        compiler_params=pltpu.CompilerParams(vmem_limit_bytes=VMEM_LIMIT),
        cost_estimate=pl.CostEstimate(
            flops=rows * full * 12, bytes_accessed=rows * full * 16, transcendentals=0
        ),
    )(core.reshape(1), own, come, moment, second)


def local(tokens, latent_rows, dec_bias, enc_rows, latent_encoder_bias, dec_rows, enc_m, enc_v, dec_m, dec_v):
    me = lax.axis_index("lat")
    core = me % 2
    tok_dev, full = tokens.shape
    row_count = enc_rows.shape[0]
    half = full // 2
    mine, other = core * half, (1 - core) * half
    first_wid = (lax.axis_index("wid") == 0).astype(jnp.int32)
    ids = jnp.stack([me, me ^ 1, first_wid]).astype(jnp.int32)

    info = jnp.concatenate(
        [
            (latent_rows // row_count).astype(BF16),
            (latent_rows % row_count).astype(BF16),
            jnp.zeros((tok_dev, 128 - 2 * latent_rows.shape[1]), BF16),
        ],
        axis=1,
    )
    cut = lambda a, at: lax.dynamic_slice_in_dim(a, at, half, axis=a.ndim - 1)
    own_part = jnp.concatenate([cut(tokens, mine), info], axis=1)
    come_part = core_swap(jnp.concatenate([cut(tokens, other), info], axis=1))
    even = core == 0
    unit = jnp.concatenate(
        [jnp.where(even, own_part, come_part), jnp.where(even, come_part, own_part)], axis=0
    )
    near = [unit] + [plane_shift(unit, dx, 0) for dx in (1, -1, 2)]
    enc_rows, dec_rows = lax.optimization_barrier((enc_rows, dec_rows, unit))[:2]
    bias_half = cut(dec_bias, mine).reshape(1, half)
    row_bias = latent_encoder_bias.reshape(1, row_count)
    enc_own, dec_own = cut(enc_rows, mine), cut(dec_rows, mine)
    enc_other, dec_other = core_swap(cut(enc_rows, other)), core_swap(cut(dec_rows, other))
    part = half // 2
    homes = [jnp.concatenate([v[:, cols] for v in near], axis=0) for cols in (slice(0, part), slice(part, None))]
    homes[0] = tie(homes[0], enc_own, enc_other, dec_own, dec_other)

    group_tok = homes[0].shape[0]
    unit_tok = group_tok // NX
    slots = group_tok // tok_dev * CAP
    flops = 2 * group_tok * 2 * row_count * half
    xs, metas = {}, {}

    def encode(gs, parts):
        vals, *found = whole(
            functools.partial(encode_kernel, len(gs)),
            [shape(2, len(gs), slots)] + [shape(group_tok + slots, 128, kind=BF16)] * len(gs),
            parts + [bias_half, enc_own, enc_other, row_bias],
            scalars=ids,
            flops=3 * flops * len(gs),
        )
        for k, g in enumerate(gs):
            xs[g], metas[g] = parts[2 * k : 2 * k + 2], found[k]
        return vals

    pre = wid_core_sum(jnp.concatenate(z_gather(homes, encode), axis=1))

    def recon(g, h, come, kinds=(BF16,)):
        return whole(
            functools.partial(recon_kernel, len(come), g, h),
            [shape(group_tok, part, kind=k) for k in kinds],
            [pre, metas[g], dec_own, dec_other] + come,
            flops=flops,
        )

    ups, downs = [None, None], [None, None]
    for step in range(NZ // 2):
        for h in range(2):
            for way, chain, odd in ((-1, ups, 1), (1, downs, 0)):
                if step == 0:
                    if h == 1 - odd:
                        chain[h] = recon(NZ - 1, h, [])[0]
                else:
                    g = NZ - 1 - 2 * step if odd else NZ - 2 * step
                    come = [] if chain[h] is None else [plane_shift(chain[h], 0, way)]
                    chain[h] = recon(g, h, come)[0]
    errs = []
    for h in range(2):
        come = [plane_shift(ups[h], 0, -1), plane_shift(downs[h], 0, 1)]
        exact, sent = recon(0, h, come, (F32, BF16))
        right, left = plane_shift(sent, 1, 0), plane_shift(sent, -1, 0)
        far_right = plane_shift(right[: 2 * unit_tok], 1, 0)
        far_left = plane_shift(left[2 * unit_tok :], -1, 0)
        errs += whole(
            functools.partial(err_kernel, h),
            [shape(group_tok, part, kind=BF16)],
            [exact, right, left, far_right, far_left, homes[h], bias_half],
        )

    grads = []

    def inner(gs, parts):
        held = list(grads)
        n = len(gs)
        value, *grads[:] = whole(
            functools.partial(inner_kernel, gs, not held),
            [shape(2, n, slots)] + [shape(row_count, half)] * 2,
            parts + [metas[g] for g in gs] + [pre, dec_own, dec_other] + held,
            flops=4 * flops * n,
            aliases={3 * n + 3: 1, 3 * n + 4: 2} if held else None,
        )
        return value

    dz = wid_core_sum(jnp.concatenate(z_gather(errs, inner), axis=1))
    sources = [a for g in range(NZ) for a in xs[g] + [metas[g]]]
    vm, anywhere = pl.BlockSpec(memory_space=pltpu.VMEM), pl.BlockSpec(memory_space=pl.ANY)
    enc_mine, enc_away = pl.pallas_call(
        functools.partial(enc_grad_kernel, NZ),
        out_shape=(shape(row_count, half),) * 2,
        in_specs=[vm, vm] + [anywhere] * len(sources),
        out_specs=(vm, vm),
        scratch_shapes=[pltpu.VMEM((NZ,) + a.shape, BF16) for a in sources[:3]]
        + [pltpu.SemaphoreType.DMA((3 * NZ,))],
        compiler_params=pltpu.CompilerParams(vmem_limit_bytes=VMEM_LIMIT),
        cost_estimate=pl.CostEstimate(flops=16 * flops, bytes_accessed=5_000_000, transcendentals=0),
    )(dz, bias_half, *sources)
    dec_step, dec_m_new, dec_v_new = adam(core, grads[0], core_swap(grads[1]), dec_m, dec_v)
    enc_step, enc_m_new, enc_v_new = adam(core, enc_mine, core_swap(enc_away), enc_m, enc_v)
    return (enc_step, dec_step, enc_m_new, enc_v_new, dec_m_new, dec_v_new)


def solution(mesh):
    grid = P("lat", "wid")
    return jax.shard_map(
        local,
        mesh=mesh,
        in_specs=(grid, P("lat", None), P("wid"), grid, P("lat"), grid, grid, grid, grid, grid),
        out_specs=(grid,) * 6,
        check_vma=False,
    )
```

```python
import functools

import jax
import jax.numpy as jnp
from jax import lax
from jax.experimental import pallas as pl
from jax.experimental.pallas import tpu as pltpu
from jax.sharding import PartitionSpec as P

F32 = jnp.float32
BF16 = jnp.bfloat16
NX, NZ = 4, 8
CAP = 24
VMEM_LIMIT = 12 * 1024 * 1024
FROM = {1: (1, 3, 0, 2), -1: (2, 0, 3, 1), 2: (3, 2, 1, 0)}


def plane_shift(value, dx, dz):
    pairs = []
    for i in range(2 * NX * NZ):
        x, z, core = i // (2 * NZ), (i // 2) % NZ, i % 2
        pairs.append((i, (((x + dx) % NX) * NZ + (z + dz) % NZ) * 2 + core))
    return lax.ppermute(value, "lat", pairs)


def core_swap(value):
    return lax.ppermute(value, "lat", [(i, i ^ 1) for i in range(2 * NX * NZ)])


def tie(first, *rest):
    return lax.optimization_barrier((first, *rest))[0]


def z_gather(home, work):
    up = down = home
    half = home.shape[0] // 2
    out = [work([0], [[home]])]
    for step in range(NZ // 2):
        if step:
            up = tie(up, *jax.tree.leaves(out[-2]))
        if step < NZ // 2 - 1:
            up, down = plane_shift(up, 0, 1), plane_shift(down, 0, -1)
            out.append(work([2 * step + 1, 2 * step + 2], [[up], [down]]))
        else:
            far = [plane_shift(up[:half], 0, 1), plane_shift(down[half:], 0, -1)]
            out.append(work([NZ - 1], [far]))
    return out[-1]


def dot(a, b, dims):
    return lax.dot_general(a, b, (dims, ((), ())), preferred_element_type=F32)


def pick(dense, spread, rows_hot):
    high = dense.astype(BF16)
    low = (dense - high.astype(F32)).astype(BF16)
    by_slot = dot(high, rows_hot, ((1,), (1,))) + dot(low, rows_hot, ((1,), (1,)))
    return jnp.sum(by_slot * spread.astype(F32), axis=0, keepdims=True)


def flag(mask):
    return mask.astype(F32).astype(BF16)


def iota(dims, axis):
    return lax.broadcasted_iota(jnp.int32, dims, axis)


def hots(meta, o, tokens, row_count):
    slots = meta.shape[0] - tokens
    start = meta[:tokens, 2 * o : 2 * o + 1].astype(F32)
    end = meta[:tokens, 2 * o + 1 : 2 * o + 2].astype(F32)
    lane = iota((tokens, slots), 1).astype(F32)
    row = meta[tokens:, o : o + 1].astype(F32)
    row_one = iota((slots, row_count), 1).astype(F32) + 1.0
    return flag((lane >= start) & (lane < end)), flag(row == row_one)


def center(x, bias):
    return (x.astype(F32) - bias.astype(F32)).astype(BF16)


def joined(refs, cols=slice(None)):
    parts = [ref[:, cols] for ref in refs]
    return parts[0] if len(parts) == 1 else jnp.concatenate(parts, axis=0)


def take(refs, counts):
    refs, groups = list(refs), []
    for c in counts:
        groups.append(refs[:c])
        refs = refs[c:]
    return groups, refs


def encode_kernel(gs, counts, first, ids, *refs):
    n = len(gs)
    xs, refs = take(refs, counts)
    bias_ref, own_ref, other_ref, row_bias_ref = refs[:4]
    val_ref, metas = refs[-n - 1], refs[-n:]
    row_count, width = own_ref.shape
    tokens = sum(r.shape[0] for r in xs[0])
    slots = metas[0].shape[0] - tokens
    block = tokens * CAP // slots
    lane = iota((tokens, 128), 1)
    before = flag(iota((128, 128), 0) < iota((128, 128), 1))
    t_row, t_col = iota((tokens, tokens), 0), iota((tokens, tokens), 1)
    earlier = flag((t_col < t_row) & (t_col // block == t_row // block))
    ones = jnp.ones((128, slots), BF16)
    base = (iota((tokens, slots), 0) // block * CAP).astype(F32)
    slot_lane = iota((tokens, slots), 1).astype(F32)
    slot_one = iota((slots, 128), 0).astype(F32) + 1.0
    row_one = iota((slots, row_count), 1).astype(F32) + 1.0
    jobs = [(k, o) for k in range(n) for o in range(2)]
    infos = [joined(x, slice(width, width + 128)).astype(F32) for x in xs]
    loc_ones = [pltpu.roll(info, 96, axis=1) + 1.0 for info in infos]
    owned = [(infos[k] == ids[o].astype(F32)) & (lane < 32) for k, o in jobs]
    owned_b = [flag(w) for w in owned]
    count = [dot(w, ones, ((1,), (0,))) for w in owned_b]
    in_token = [dot(w, before, ((1,), (0,))) for w in owned_b]
    start = [base + dot(earlier, c.astype(BF16), ((1,), (0,))) for c in count]
    end = [s + c for s, c in zip(start, count)]
    spread = [flag((slot_lane >= s) & (slot_lane < e)) for s, e in zip(start, end)]
    number = [
        jnp.where(w, s[:, :128] + i + 1.0, 0.0).astype(BF16) for w, s, i in zip(owned, start, in_token)
    ]
    place = [jnp.where(w, loc_ones[k], 0.0).astype(BF16) for w, (k, o) in zip(owned, jobs)]
    slot_number = [dot(s, v, ((0,), (0,))) for s, v in zip(spread, number)]
    slot_place = [dot(s, v, ((0,), (0,))) for s, v in zip(spread, place)]
    row = [
        jnp.sum(jnp.where(v == slot_one, p, 0.0), axis=1, keepdims=True)
        for v, p in zip(slot_number, slot_place)
    ]
    centered = [center(joined(x, slice(0, width)), bias_ref[...]) for x in xs]
    for j, (k, o) in enumerate(jobs):
        rows = own_ref if o == 0 else other_ref
        dense = dot(centered[k], rows[...], ((1,), (1,)))
        if o == 0:
            dense = dense + row_bias_ref[...] * ids[2].astype(F32)
        val_ref[o, gs[k] : gs[k] + 1, :] = pick(dense, spread[j], flag(row[j] == row_one))
    slot_lane_128 = iota((slots, 128), 1)
    for k in range(n):
        s0, s1, e0, e1 = (v[2 * k + o][:, :128] for v in (start, end) for o in range(2))
        by_token = jnp.where(lane == 0, s0, jnp.where(lane == 1, e0, jnp.where(lane == 2, s1, e1)))
        metas[k][:tokens, :] = by_token.astype(BF16)
        metas[k][tokens:, :] = jnp.where(slot_lane_128 == 0, row[2 * k], row[2 * k + 1]).astype(BF16)


def select_kernel(counts, row_count, *refs):
    n = len(counts)
    xs, refs = take(refs, counts)
    metas, bias_ref, outs = refs[:n], refs[n], refs[n + 1 : 2 * n + 1]
    buffer, sems = refs[2 * n + 1 :]
    width = bias_ref.shape[1]
    copies = []
    for k in range(n):
        x = center(joined(xs[k], slice(0, width)), bias_ref[...])
        meta = metas[k][...]
        tokens = x.shape[0]
        for o in range(2):
            spread, _ = hots(meta, o, tokens, row_count)
            buffer[k, o, :, :width] = dot(spread, x, ((0,), (0,))).astype(BF16)
            buffer[k, o, :, width:] = meta[tokens:, :]
            copies.append(pltpu.make_async_copy(buffer.at[k, o], outs[k].at[o], sems.at[k, o]))
            copies[-1].start()
    for copy in copies:
        copy.wait()


def column(values):
    return jnp.transpose(jnp.broadcast_to(values, (8, values.shape[1])))[:, :1]


def recon_kernel(offsets, g, *refs):
    val_ref, meta_ref, own_ref, other_ref = refs[:4]
    come, outs = refs[4 : 4 + len(offsets)], refs[4 + len(offsets) :]
    slots = val_ref.shape[2]
    tokens = meta_ref.shape[0] - slots
    meta = meta_ref[...]
    total = None
    for o in range(2):
        spread, hot = hots(meta, o, tokens, own_ref.shape[0])
        rows = dot(hot, (own_ref if o == 0 else other_ref)[...], ((1,), (0,)))
        contrib = (column(val_ref[o, g : g + 1, :]) * rows).astype(BF16)
        term = dot(spread, contrib, ((1,), (0,)))
        total = term if total is None else total + term
    if offsets and come[0].shape[0] < tokens:
        at, part = offsets[0], come[0].shape[0]
        added = total[at : at + part] + come[0][...].astype(F32)
        total = jnp.concatenate([added, total[part:]] if at == 0 else [total[:at], added], axis=0)
    else:
        for c in come:
            total = total + c[...].astype(F32)
    if outs[0].shape[0] < tokens:
        part = outs[0].shape[0]
        for k, out in enumerate(outs):
            out[...] = total[k * part : (k + 1) * part].astype(out.dtype)
    else:
        for out in outs:
            out[...] = total.astype(out.dtype)


def err_kernel(sum_ref, up_ref, down_ref, far_up_ref, far_down_ref, x_ref, bias_ref, err_ref):
    tokens, width = err_ref.shape
    unit = tokens // NX
    piece = lambda ref, k: ref[k * unit : (k + 1) * unit, :].astype(F32)
    for k in range(NX):
        total = piece(sum_ref, k)
        total = total + piece(up_ref, FROM[1].index(k))
        total = total + piece(down_ref, FROM[-1].index(k))
        far = FROM[2].index(k)
        total = total + (piece(far_up_ref, far) if far < 2 else piece(far_down_ref, far - 2))
        recon = bias_ref[...].astype(F32) + total
        raw = x_ref[k * unit : (k + 1) * unit, :width].astype(F32)
        err_ref[k * unit : (k + 1) * unit, :] = (recon - raw).astype(BF16)


def inner_kernel(gs, counts, first, *refs):
    n = len(gs)
    errs, refs = take(refs, counts)
    metas, (pre_ref, own_ref, other_ref) = refs[:n], refs[n : n + 3]
    held, (val_ref, *grads) = refs[n + 3 : -3], refs[-3:]
    row_count = own_ref.shape[0]
    es = [joined(e) for e in errs]
    tokens = es[0].shape[0]
    for o in range(2):
        rows = own_ref if o == 0 else other_ref
        total = None
        for k, g in enumerate(gs):
            spread, hot = hots(metas[k][...], o, tokens, row_count)
            val_ref[o, g : g + 1, :] = pick(dot(es[k], rows[...], ((1,), (1,))), spread, hot)
            by_slot = dot(spread, es[k], ((0,), (0,)))
            term = (column(pre_ref[o, g : g + 1, :]) * by_slot).astype(BF16)
            grad = dot(hot, term, ((0,), (0,)))
            total = grad if total is None else total + grad
        grads[o][...] = total if first else held[1 + o][...] + total


def enc_grad_kernel(n, o, val_ref, *refs):
    sources, out, buffer, sems = refs[:n], refs[n], refs[n + 1], refs[n + 2]
    copies = [pltpu.make_async_copy(s.at[o], buffer.at[g], sems.at[g]) for g, s in enumerate(sources)]
    for copy in copies:
        copy.start()
    values = jnp.transpose(val_ref[o])
    row_count, width = out.shape
    slots = buffer.shape[1]
    row_one = iota((slots, row_count), 1).astype(F32) + 1.0
    total = None
    for g in range(n):
        copies[g].wait()
        term = (values[:, g : g + 1] * buffer[g, :, :width].astype(F32)).astype(BF16)
        row = buffer[g, :, width : width + 128][:, o : o + 1].astype(F32)
        grad = dot(flag(row == row_one), term, ((0,), (0,)))
        total = grad if total is None else total + grad
    out[...] = total


def adam_kernel(ids, own_ref, come_ref, m_ref, v_ref, step_ref, m_out, v_out):
    mine = pl.program_id(1) == ids[0]
    grad = jnp.where(mine, own_ref[...], come_ref[...])
    first = 0.9 * m_ref[...].astype(F32) + 0.1 * grad
    second = 0.95 * v_ref[...].astype(F32) + 0.05 * grad * grad
    scale = 1.0 / (1.0 - 0.9**10)
    step_ref[...] = first * scale / (jnp.sqrt(second * (1.0 / (1.0 - 0.95**10))) + 1e-08)
    m_out[...] = first.astype(BF16)
    v_out[...] = second.astype(BF16)


def whole(kernel, outs, args, scalars=None, flops=0, aliases=None):
    vm = pl.BlockSpec(memory_space=pltpu.VMEM)
    sm = pl.BlockSpec(memory_space=pltpu.SMEM)
    specs = ([sm] if scalars is not None else []) + [vm] * len(args)
    size = sum(a.size * a.dtype.itemsize for a in args) + sum(
        o.size * o.dtype.itemsize for o in outs
    )
    call = pl.pallas_call(
        kernel,
        out_shape=tuple(outs),
        in_specs=specs,
        out_specs=(vm,) * len(outs),
        input_output_aliases=aliases or {},
        compiler_params=pltpu.CompilerParams(vmem_limit_bytes=VMEM_LIMIT),
        cost_estimate=pl.CostEstimate(flops=flops, bytes_accessed=size, transcendentals=0),
    )
    return call(*(([scalars] if scalars is not None else []) + list(args)))


def shape(*dims, kind=F32):
    return jax.ShapeDtypeStruct(dims, kind)


def wid_core_sum(values):
    values = values + core_swap(values)[::-1]
    for pairs in ([(0, 1), (1, 0), (2, 3), (3, 2)], [(0, 3), (3, 0), (1, 2), (2, 1)]):
        values = values + lax.ppermute(values, "wid", pairs)
    return values


def adam(core, own, come, moment, second):
    rows, full = moment.shape
    half = full // 2
    tile = rows // 2
    half_spec = pl.BlockSpec((tile, half), lambda i, h, ids: (i, 0))
    full_spec = pl.BlockSpec((tile, half), lambda i, h, ids: (i, h))
    return pl.pallas_call(
        adam_kernel,
        out_shape=(shape(rows, full), shape(rows, full, kind=BF16), shape(rows, full, kind=BF16)),
        grid_spec=pltpu.PrefetchScalarGridSpec(
            num_scalar_prefetch=1,
            grid=(rows // tile, 2),
            in_specs=[half_spec, half_spec, full_spec, full_spec],
            out_specs=(full_spec, full_spec, full_spec),
        ),
        compiler_params=pltpu.CompilerParams(vmem_limit_bytes=VMEM_LIMIT),
        cost_estimate=pl.CostEstimate(
            flops=rows * full * 12, bytes_accessed=rows * full * 16, transcendentals=0
        ),
    )(core.reshape(1), own, come, moment, second)


def local(tokens, latent_rows, dec_bias, enc_rows, latent_encoder_bias, dec_rows, enc_m, enc_v, dec_m, dec_v):
    me = lax.axis_index("lat")
    core = me % 2
    tok_dev, full = tokens.shape
    row_count = enc_rows.shape[0]
    half = full // 2
    mine, other = core * half, (1 - core) * half
    first_wid = (lax.axis_index("wid") == 0).astype(jnp.int32)
    ids = jnp.stack([me, me ^ 1, first_wid]).astype(jnp.int32)

    info = jnp.concatenate(
        [
            (latent_rows // row_count).astype(BF16),
            (latent_rows % row_count).astype(BF16),
            jnp.zeros((tok_dev, 128 - 2 * latent_rows.shape[1]), BF16),
        ],
        axis=1,
    )
    cut = lambda a, at: lax.dynamic_slice_in_dim(a, at, half, axis=a.ndim - 1)
    own_part = jnp.concatenate([cut(tokens, mine), info], axis=1)
    come_part = core_swap(jnp.concatenate([cut(tokens, other), info], axis=1))
    even = core == 0
    unit = jnp.concatenate(
        [jnp.where(even, own_part, come_part), jnp.where(even, come_part, own_part)], axis=0
    )
    near = [unit] + [plane_shift(unit, dx, 0) for dx in (1, -1, 2)]
    enc_rows, dec_rows = lax.optimization_barrier((enc_rows, dec_rows, unit))[:2]
    bias_half = cut(dec_bias, mine).reshape(1, half)
    row_bias = latent_encoder_bias.reshape(1, row_count)
    enc_own, dec_own = cut(enc_rows, mine), cut(dec_rows, mine)
    enc_other, dec_other = core_swap(cut(enc_rows, other)), core_swap(cut(dec_rows, other))
    home = tie(jnp.concatenate(near, axis=0), enc_own, enc_other, dec_own, dec_other)

    group_tok = home.shape[0]
    slots = group_tok // tok_dev * CAP
    flops = 2 * group_tok * 2 * row_count * half
    xs, metas = {}, {}
    vals_shape = shape(2, NZ, slots)

    def encode(gs, groups, held=[]):
        n = len(gs)
        args = [part for x in groups for part in x] + [bias_half, enc_own, enc_other, row_bias]
        held[:], found = (
            lambda out: (out[:1], out[1:])
        )(
            whole(
                functools.partial(encode_kernel, gs, [len(x) for x in groups], not held),
                [vals_shape] + [shape(group_tok + slots, 128, kind=BF16)] * n,
                args + held,
                scalars=ids,
                flops=3 * flops * n,
                aliases={len(args) + 1: 0} if held else None,
            )
        )
        for k, g in enumerate(gs):
            xs[g], metas[g] = groups[k], found[k]
        return list(held)

    pre = wid_core_sum(z_gather(home, functools.partial(encode, held=[]))[0])

    def recon(g, come=(), offsets=(), kinds=(BF16,), rows=group_tok):
        return whole(
            functools.partial(recon_kernel, offsets or (0,) * len(come), g),
            [shape(rows, half, kind=k) for k in kinds],
            [pre, metas[g], dec_own, dec_other] + list(come),
            flops=2 * flops,
        )

    vm, far_memory = pl.BlockSpec(memory_space=pltpu.VMEM), pl.BlockSpec(memory_space=pltpu.HBM)

    def select(gs, after):
        args = [part for g in gs for part in xs[g]] + [tie(metas[g], after) for g in gs] + [bias_half]
        out = shape(2, slots, half + 128, kind=BF16)
        return pl.pallas_call(
            functools.partial(select_kernel, [len(xs[g]) for g in gs], row_count),
            out_shape=(out,) * len(gs),
            in_specs=[vm] * len(args),
            out_specs=(far_memory,) * len(gs),
            scratch_shapes=[
                pltpu.VMEM((len(gs),) + out.shape, BF16),
                pltpu.SemaphoreType.DMA((len(gs), 2)),
            ],
            compiler_params=pltpu.CompilerParams(vmem_limit_bytes=VMEM_LIMIT),
            cost_estimate=pl.CostEstimate(flops=2 * flops, bytes_accessed=2_500_000, transcendentals=0),
        )(*args)

    half_rows = group_tok // 2
    up, down = recon(NZ - 1, kinds=(BF16, BF16), rows=half_rows)
    chosen = []
    for step in range(1, NZ // 2):
        picked = select([2 * step - 2, 2 * step - 1], up)
        offsets = ((0,), (half_rows,)) if step == 1 else ((0,), (0,))
        come_up, come_down = plane_shift(up, 0, -1), plane_shift(down, 0, 1)
        (up,) = recon(NZ - 1 - 2 * step, [come_up], offsets[0])
        (down,) = recon(NZ - 2 * step, [come_down], offsets[1])
        chosen += picked
        up = tie(up, *picked)
    last = select([NZ - 2, NZ - 1], up)
    chosen += last
    come = [plane_shift(up, 0, -1), plane_shift(down, 0, 1)]
    exact, sent = recon(0, come, kinds=(F32, BF16))
    sent = tie(sent, *last)
    right, left = plane_shift(sent, 1, 0), plane_shift(sent, -1, 0)
    far_right, far_left = plane_shift(right[:half_rows], 1, 0), plane_shift(left[half_rows:], -1, 0)
    (err_home,) = whole(
        err_kernel,
        [shape(group_tok, half, kind=BF16)],
        [exact, right, left, far_right, far_left, home, bias_half],
    )

    def inner(gs, groups, held):
        args = [part for e in groups for part in e] + [metas[g] for g in gs] + [pre, dec_own, dec_other]
        m = len(args)
        held[:] = whole(
            functools.partial(inner_kernel, gs, [len(e) for e in groups], not held),
            [vals_shape] + [shape(row_count, half)] * 2,
            args + held,
            flops=4 * flops * len(gs),
            aliases={m: 0, m + 1: 1, m + 2: 2} if held else None,
        )
        return list(held)

    products, *grads = z_gather(err_home, functools.partial(inner, held=[]))
    dz = wid_core_sum(products)
    enc_away, enc_mine = [
        pl.pallas_call(
            functools.partial(enc_grad_kernel, NZ, o),
            out_shape=shape(row_count, half),
            in_specs=[vm] + [far_memory] * NZ,
            out_specs=vm,
            scratch_shapes=[
                pltpu.VMEM((NZ, slots, half + 128), BF16),
                pltpu.SemaphoreType.DMA((NZ,)),
            ],
            compiler_params=pltpu.CompilerParams(vmem_limit_bytes=VMEM_LIMIT),
            cost_estimate=pl.CostEstimate(flops=8 * flops, bytes_accessed=5_000_000, transcendentals=0),
        )(dz, *chosen)
        for o in (1, 0)
    ]
    dec_step, dec_m_new, dec_v_new = adam(core, grads[0], core_swap(grads[1]), dec_m, dec_v)
    enc_step, enc_m_new, enc_v_new = adam(core, enc_mine, core_swap(enc_away), enc_m, enc_v)
    return (enc_step, dec_step, enc_m_new, enc_v_new, dec_m_new, dec_v_new)


def solution(mesh):
    grid = P("lat", "wid")
    return jax.shard_map(
        local,
        mesh=mesh,
        in_specs=(grid, P("lat", None), P("wid"), grid, P("lat"), grid, grid, grid, grid, grid),
        out_specs=(grid,) * 6,
        check_vma=False,
    )
```

```python
import functools

import jax
import jax.numpy as jnp
from jax import lax
from jax.experimental import pallas as pl
from jax.experimental.pallas import tpu as pltpu
from jax.sharding import PartitionSpec as P

F32 = jnp.float32
BF16 = jnp.bfloat16
NX, NZ = 4, 8
CAP = 24
VMEM_LIMIT = 12 * 1024 * 1024
FROM = {1: (1, 3, 0, 2), -1: (2, 0, 3, 1), 2: (3, 2, 1, 0)}


def plane_shift(value, dx, dz):
    return turned_shift(value, dx, dz, 1)


def turned_shift(value, dx, dz, turn=-1):
    pairs = []
    for i in range(2 * NX * NZ):
        x, z, core = i // (2 * NZ), (i // 2) % NZ, i % 2
        way = turn if core else 1
        pairs.append((i, (((x + way * dx) % NX) * NZ + (z + way * dz) % NZ) * 2 + core))
    return lax.ppermute(value, "lat", pairs)


def core_swap(value):
    return lax.ppermute(value, "lat", [(i, i ^ 1) for i in range(2 * NX * NZ)])


def tie(first, *rest):
    return lax.optimization_barrier((first, *rest))[0]


def z_gather(home, work):
    up = down = home
    half = home.shape[0] // 2
    out = [work([0], [[home]])]
    for step in range(NZ // 2):
        if step:
            up = tie(up, *jax.tree.leaves(out[-2]))
        if step < NZ // 2 - 1:
            up, down = turned_shift(up, 0, 1), turned_shift(down, 0, -1)
            out.append(work([2 * step + 1, 2 * step + 2], [[up], [down]]))
        else:
            far = [turned_shift(up[:half], 0, 1), turned_shift(down[half:], 0, -1)]
            out.append(work([NZ - 1], [far]))
    return out[-1]


def dot(a, b, dims):
    return lax.dot_general(a, b, (dims, ((), ())), preferred_element_type=F32)


def pick(dense, spread, rows_hot):
    high = dense.astype(BF16)
    low = (dense - high.astype(F32)).astype(BF16)
    by_slot = dot(high, rows_hot, ((1,), (1,))) + dot(low, rows_hot, ((1,), (1,)))
    return jnp.sum(by_slot * spread.astype(F32), axis=0, keepdims=True)


def flag(mask):
    return mask.astype(F32).astype(BF16)


def iota(dims, axis):
    return lax.broadcasted_iota(jnp.int32, dims, axis)


def hots(meta, o, tokens, row_count):
    slots = meta.shape[0] - tokens
    start = meta[:tokens, 2 * o : 2 * o + 1].astype(F32)
    end = meta[:tokens, 2 * o + 1 : 2 * o + 2].astype(F32)
    lane = iota((tokens, slots), 1).astype(F32)
    row = meta[tokens:, o : o + 1].astype(F32)
    row_one = iota((slots, row_count), 1).astype(F32) + 1.0
    return flag((lane >= start) & (lane < end)), flag(row == row_one)


def center(x, bias):
    return (x.astype(F32) - bias.astype(F32)).astype(BF16)


def joined(refs, cols=slice(None)):
    parts = [ref[:, cols] for ref in refs]
    return parts[0] if len(parts) == 1 else jnp.concatenate(parts, axis=0)


def take(refs, counts):
    refs, groups = list(refs), []
    for c in counts:
        groups.append(refs[:c])
        refs = refs[c:]
    return groups, refs


def place_of(ids, g):
    if g in (0, NZ - 1):
        return pl.ds(g, 1)
    return pl.ds(g + lax.rem(ids[0], 2) * (1 if g % 2 else -1), 1)


def encode_kernel(gs, counts, first, ids, *refs):
    n = len(gs)
    xs, refs = take(refs, counts)
    bias_ref, own_ref, other_ref, row_bias_ref = refs[:4]
    val_ref, metas = refs[-n - 1], refs[-n:]
    row_count, width = own_ref.shape
    tokens = sum(r.shape[0] for r in xs[0])
    slots = metas[0].shape[0] - tokens
    block = tokens * CAP // slots
    lane = iota((tokens, 128), 1)
    before = flag(iota((128, 128), 0) < iota((128, 128), 1))
    t_row, t_col = iota((tokens, tokens), 0), iota((tokens, tokens), 1)
    earlier = flag((t_col < t_row) & (t_col // block == t_row // block))
    ones = jnp.ones((128, slots), BF16)
    base = (iota((tokens, slots), 0) // block * CAP).astype(F32)
    slot_lane = iota((tokens, slots), 1).astype(F32)
    slot_one = iota((slots, 128), 0).astype(F32) + 1.0
    row_one = iota((slots, row_count), 1).astype(F32) + 1.0
    jobs = [(k, o) for k in range(n) for o in range(2)]
    infos = [joined(x, slice(width, width + 128)).astype(F32) for x in xs]
    loc_ones = [pltpu.roll(info, 96, axis=1) + 1.0 for info in infos]
    owned = [(infos[k] == ids[o].astype(F32)) & (lane < 32) for k, o in jobs]
    owned_b = [flag(w) for w in owned]
    count = [dot(w, ones, ((1,), (0,))) for w in owned_b]
    in_token = [dot(w, before, ((1,), (0,))) for w in owned_b]
    start = [base + dot(earlier, c.astype(BF16), ((1,), (0,))) for c in count]
    end = [s + c for s, c in zip(start, count)]
    spread = [flag((slot_lane >= s) & (slot_lane < e)) for s, e in zip(start, end)]
    number = [
        jnp.where(w, s[:, :128] + i + 1.0, 0.0).astype(BF16) for w, s, i in zip(owned, start, in_token)
    ]
    place = [jnp.where(w, loc_ones[k], 0.0).astype(BF16) for w, (k, o) in zip(owned, jobs)]
    slot_number = [dot(s, v, ((0,), (0,))) for s, v in zip(spread, number)]
    slot_place = [dot(s, v, ((0,), (0,))) for s, v in zip(spread, place)]
    row = [
        jnp.sum(jnp.where(v == slot_one, p, 0.0), axis=1, keepdims=True)
        for v, p in zip(slot_number, slot_place)
    ]
    centered = [center(joined(x, slice(0, width)), bias_ref[...]) for x in xs]
    for j, (k, o) in enumerate(jobs):
        rows = own_ref if o == 0 else other_ref
        dense = dot(centered[k], rows[...], ((1,), (1,)))
        if o == 0:
            dense = dense + row_bias_ref[...] * ids[2].astype(F32)
        val_ref[o, place_of(ids, gs[k]), :] = pick(dense, spread[j], flag(row[j] == row_one))
    slot_lane_128 = iota((slots, 128), 1)
    for k in range(n):
        s0, s1, e0, e1 = (v[2 * k + o][:, :128] for v in (start, end) for o in range(2))
        by_token = jnp.where(lane == 0, s0, jnp.where(lane == 1, e0, jnp.where(lane == 2, s1, e1)))
        metas[k][:tokens, :] = by_token.astype(BF16)
        metas[k][tokens:, :] = jnp.where(slot_lane_128 == 0, row[2 * k], row[2 * k + 1]).astype(BF16)


def select_kernel(counts, row_count, *refs):
    n = len(counts)
    xs, refs = take(refs, counts)
    metas, bias_ref, outs = refs[:n], refs[n], refs[n + 1 : 2 * n + 1]
    buffer, sems = refs[2 * n + 1 :]
    width = bias_ref.shape[1]
    copies = []
    for k in range(n):
        x = center(joined(xs[k], slice(0, width)), bias_ref[...])
        meta = metas[k][...]
        tokens = x.shape[0]
        for o in range(2):
            spread, _ = hots(meta, o, tokens, row_count)
            buffer[k, o, :, :width] = dot(spread, x, ((0,), (0,))).astype(BF16)
            buffer[k, o, :, width:] = meta[tokens:, :]
            copies.append(pltpu.make_async_copy(buffer.at[k, o], outs[k].at[o], sems.at[k, o]))
            copies[-1].start()
    for copy in copies:
        copy.wait()


def column(values):
    return jnp.transpose(jnp.broadcast_to(values, (8, values.shape[1])))[:, :1]


def recon_kernel(offsets, g, ids, *refs):
    val_ref, meta_ref, own_ref, other_ref = refs[:4]
    come, outs = refs[4 : 4 + len(offsets)], refs[4 + len(offsets) :]
    slots = val_ref.shape[2]
    tokens = meta_ref.shape[0] - slots
    meta = meta_ref[...]
    total = None
    for o in range(2):
        spread, hot = hots(meta, o, tokens, own_ref.shape[0])
        rows = dot(hot, (own_ref if o == 0 else other_ref)[...], ((1,), (0,)))
        contrib = (column(val_ref[o, place_of(ids, g), :]) * rows).astype(BF16)
        term = dot(spread, contrib, ((1,), (0,)))
        total = term if total is None else total + term
    if offsets and come[0].shape[0] < tokens:
        at, part = offsets[0], come[0].shape[0]
        added = total[at : at + part] + come[0][...].astype(F32)
        total = jnp.concatenate([added, total[part:]] if at == 0 else [total[:at], added], axis=0)
    else:
        for c in come:
            total = total + c[...].astype(F32)
    if outs[0].shape[0] < tokens:
        part = outs[0].shape[0]
        for k, out in enumerate(outs):
            out[...] = total[k * part : (k + 1) * part].astype(out.dtype)
    else:
        for out in outs:
            out[...] = total.astype(out.dtype)


def err_kernel(ids, sum_ref, up_ref, down_ref, far_up_ref, far_down_ref, x_ref, bias_ref, err_ref):
    tokens, width = err_ref.shape
    unit = tokens // NX
    piece = lambda ref, k: ref[k * unit : (k + 1) * unit, :].astype(F32)
    for k in range(NX):
        total = piece(sum_ref, k)
        here, there = FROM[1].index(k), FROM[-1].index(k)
        first = piece(up_ref, here) + piece(down_ref, there)
        second = piece(down_ref, here) + piece(up_ref, there)
        total = total + jnp.where(ids[0] % 2 == 0, first, second)
        far = FROM[2].index(k)
        total = total + (piece(far_up_ref, far) if far < 2 else piece(far_down_ref, far - 2))
        recon = bias_ref[...].astype(F32) + total
        raw = x_ref[k * unit : (k + 1) * unit, :width].astype(F32)
        err_ref[k * unit : (k + 1) * unit, :] = (recon - raw).astype(BF16)


def inner_kernel(gs, counts, first, ids, *refs):
    n = len(gs)
    errs, refs = take(refs, counts)
    metas, (pre_ref, own_ref, other_ref) = refs[:n], refs[n : n + 3]
    held, (val_ref, *grads) = refs[n + 3 : -3], refs[-3:]
    row_count = own_ref.shape[0]
    es = [joined(e) for e in errs]
    tokens = es[0].shape[0]
    for o in range(2):
        rows = own_ref if o == 0 else other_ref
        total = None
        for k, g in enumerate(gs):
            spread, hot = hots(metas[k][...], o, tokens, row_count)
            val_ref[o, place_of(ids, g), :] = pick(dot(es[k], rows[...], ((1,), (1,))), spread, hot)
            by_slot = dot(spread, es[k], ((0,), (0,)))
            term = (column(pre_ref[o, place_of(ids, g), :]) * by_slot).astype(BF16)
            grad = dot(hot, term, ((0,), (0,)))
            total = grad if total is None else total + grad
        grads[o][...] = total if first else held[1 + o][...] + total


def enc_grad_kernel(n, o, ids, val_ref, *refs):
    sources, out, buffer, sems = refs[:n], refs[n], refs[n + 1], refs[n + 2]
    copies = [pltpu.make_async_copy(s.at[o], buffer.at[g], sems.at[g]) for g, s in enumerate(sources)]
    for copy in copies:
        copy.start()
    row_count, width = out.shape
    slots = buffer.shape[1]
    row_one = iota((slots, row_count), 1).astype(F32) + 1.0
    total = None
    for g in range(n):
        copies[g].wait()
        term = (column(val_ref[o, place_of(ids, g), :]) * buffer[g, :, :width].astype(F32)).astype(BF16)
        row = buffer[g, :, width : width + 128][:, o : o + 1].astype(F32)
        grad = dot(flag(row == row_one), term, ((0,), (0,)))
        total = grad if total is None else total + grad
    out[...] = total


def adam_kernel(ids, own_ref, come_ref, m_ref, v_ref, step_ref, m_out, v_out):
    mine = pl.program_id(1) == ids[0]
    grad = jnp.where(mine, own_ref[...], come_ref[...])
    first = 0.9 * m_ref[...].astype(F32) + 0.1 * grad
    second = 0.95 * v_ref[...].astype(F32) + 0.05 * grad * grad
    scale = 1.0 / (1.0 - 0.9**10)
    step_ref[...] = first * scale / (jnp.sqrt(second * (1.0 / (1.0 - 0.95**10))) + 1e-08)
    m_out[...] = first.astype(BF16)
    v_out[...] = second.astype(BF16)


def whole(kernel, outs, args, scalars=None, flops=0, aliases=None):
    vm = pl.BlockSpec(memory_space=pltpu.VMEM)
    sm = pl.BlockSpec(memory_space=pltpu.SMEM)
    specs = ([sm] if scalars is not None else []) + [vm] * len(args)
    size = sum(a.size * a.dtype.itemsize for a in args) + sum(
        o.size * o.dtype.itemsize for o in outs
    )
    call = pl.pallas_call(
        kernel,
        out_shape=tuple(outs),
        in_specs=specs,
        out_specs=(vm,) * len(outs),
        input_output_aliases=aliases or {},
        compiler_params=pltpu.CompilerParams(vmem_limit_bytes=VMEM_LIMIT),
        cost_estimate=pl.CostEstimate(flops=flops, bytes_accessed=size, transcendentals=0),
    )
    return call(*(([scalars] if scalars is not None else []) + list(args)))


def shape(*dims, kind=F32):
    return jax.ShapeDtypeStruct(dims, kind)


def wid_core_sum(values):
    values = values + core_swap(values)[::-1]
    for pairs in ([(0, 1), (1, 0), (2, 3), (3, 2)], [(0, 3), (3, 0), (1, 2), (2, 1)]):
        values = values + lax.ppermute(values, "wid", pairs)
    return values


def adam(core, own, come, moment, second):
    rows, full = moment.shape
    half = full // 2
    tile = rows // 2
    half_spec = pl.BlockSpec((tile, half), lambda i, h, ids: (i, 0))
    full_spec = pl.BlockSpec((tile, half), lambda i, h, ids: (i, h))
    return pl.pallas_call(
        adam_kernel,
        out_shape=(shape(rows, full), shape(rows, full, kind=BF16), shape(rows, full, kind=BF16)),
        grid_spec=pltpu.PrefetchScalarGridSpec(
            num_scalar_prefetch=1,
            grid=(rows // tile, 2),
            in_specs=[half_spec, half_spec, full_spec, full_spec],
            out_specs=(full_spec, full_spec, full_spec),
        ),
        compiler_params=pltpu.CompilerParams(vmem_limit_bytes=VMEM_LIMIT),
        cost_estimate=pl.CostEstimate(
            flops=rows * full * 12, bytes_accessed=rows * full * 16, transcendentals=0
        ),
    )(core.reshape(1), own, come, moment, second)


def local(tokens, latent_rows, dec_bias, enc_rows, latent_encoder_bias, dec_rows, enc_m, enc_v, dec_m, dec_v):
    me = lax.axis_index("lat")
    core = me % 2
    tok_dev, full = tokens.shape
    row_count = enc_rows.shape[0]
    half = full // 2
    mine, other = core * half, (1 - core) * half
    first_wid = (lax.axis_index("wid") == 0).astype(jnp.int32)
    ids = jnp.stack([me, me ^ 1, first_wid]).astype(jnp.int32)

    info = jnp.concatenate(
        [
            (latent_rows // row_count).astype(BF16),
            (latent_rows % row_count).astype(BF16),
            jnp.zeros((tok_dev, 128 - 2 * latent_rows.shape[1]), BF16),
        ],
        axis=1,
    )
    cut = lambda a, at: lax.dynamic_slice_in_dim(a, at, half, axis=a.ndim - 1)
    own_part = jnp.concatenate([cut(tokens, mine), info], axis=1)
    come_part = core_swap(jnp.concatenate([cut(tokens, other), info], axis=1))
    even = core == 0
    unit = jnp.concatenate(
        [jnp.where(even, own_part, come_part), jnp.where(even, come_part, own_part)], axis=0
    )
    near = [unit] + [plane_shift(unit, dx, 0) for dx in (1, -1, 2)]
    enc_rows, dec_rows = lax.optimization_barrier((enc_rows, dec_rows, unit))[:2]
    bias_half = cut(dec_bias, mine).reshape(1, half)
    row_bias = latent_encoder_bias.reshape(1, row_count)
    enc_own, dec_own = cut(enc_rows, mine), cut(dec_rows, mine)
    enc_other, dec_other = core_swap(cut(enc_rows, other)), core_swap(cut(dec_rows, other))
    home = tie(jnp.concatenate(near, axis=0), enc_own, enc_other, dec_own, dec_other)

    group_tok = home.shape[0]
    slots = group_tok // tok_dev * CAP
    flops = 2 * group_tok * 2 * row_count * half
    xs, metas = {}, {}
    vals_shape = shape(2, NZ, slots)

    def encode(gs, groups, held=[]):
        n = len(gs)
        args = [part for x in groups for part in x] + [bias_half, enc_own, enc_other, row_bias]
        held[:], found = (
            lambda out: (out[:1], out[1:])
        )(
            whole(
                functools.partial(encode_kernel, gs, [len(x) for x in groups], not held),
                [vals_shape] + [shape(group_tok + slots, 128, kind=BF16)] * n,
                args + held,
                scalars=ids,
                flops=3 * flops * n,
                aliases={len(args) + 1: 0} if held else None,
            )
        )
        for k, g in enumerate(gs):
            xs[g], metas[g] = groups[k], found[k]
        return list(held)

    pre = wid_core_sum(z_gather(home, functools.partial(encode, held=[]))[0])

    def recon(g, come=(), offsets=(), kinds=(BF16,), rows=group_tok):
        return whole(
            functools.partial(recon_kernel, offsets or (0,) * len(come), g),
            [shape(rows, half, kind=k) for k in kinds],
            [pre, metas[g], dec_own, dec_other] + list(come),
            scalars=ids,
            flops=2 * flops,
        )

    vm, far_memory = pl.BlockSpec(memory_space=pltpu.VMEM), pl.BlockSpec(memory_space=pltpu.HBM)

    def select(gs, after):
        args = [part for g in gs for part in xs[g]] + [tie(metas[g], after) for g in gs] + [bias_half]
        out = shape(2, slots, half + 128, kind=BF16)
        return pl.pallas_call(
            functools.partial(select_kernel, [len(xs[g]) for g in gs], row_count),
            out_shape=(out,) * len(gs),
            in_specs=[vm] * len(args),
            out_specs=(far_memory,) * len(gs),
            scratch_shapes=[
                pltpu.VMEM((len(gs),) + out.shape, BF16),
                pltpu.SemaphoreType.DMA((len(gs), 2)),
            ],
            compiler_params=pltpu.CompilerParams(vmem_limit_bytes=VMEM_LIMIT),
            cost_estimate=pl.CostEstimate(flops=2 * flops, bytes_accessed=2_500_000, transcendentals=0),
        )(*args)

    half_rows = group_tok // 2
    up, down = recon(NZ - 1, kinds=(BF16, BF16), rows=half_rows)
    chosen = []
    for step in range(1, NZ // 2):
        picked = select([2 * step - 2, 2 * step - 1], up)
        offsets = ((0,), (half_rows,)) if step == 1 else ((0,), (0,))
        come_up, come_down = turned_shift(up, 0, -1), turned_shift(down, 0, 1)
        (up,) = recon(NZ - 1 - 2 * step, [come_up], offsets[0])
        (down,) = recon(NZ - 2 * step, [come_down], offsets[1])
        chosen += picked
        up = tie(up, *picked)
    last = select([NZ - 2, NZ - 1], up)
    chosen += last
    come = [turned_shift(up, 0, -1), turned_shift(down, 0, 1)]
    exact, sent = recon(0, come, kinds=(F32, BF16))
    sent = tie(sent, *last)
    right, left = turned_shift(sent, 1, 0), turned_shift(sent, -1, 0)
    far_right, far_left = turned_shift(right[:half_rows], 1, 0), turned_shift(left[half_rows:], -1, 0)
    (err_home,) = whole(
        err_kernel,
        [shape(group_tok, half, kind=BF16)],
        [exact, right, left, far_right, far_left, home, bias_half],
        scalars=ids,
    )

    def inner(gs, groups, held):
        args = [part for e in groups for part in e] + [metas[g] for g in gs] + [pre, dec_own, dec_other]
        m = len(args)
        held[:] = whole(
            functools.partial(inner_kernel, gs, [len(e) for e in groups], not held),
            [vals_shape] + [shape(row_count, half)] * 2,
            args + held,
            scalars=ids,
            flops=4 * flops * len(gs),
            aliases={m + 1: 0, m + 2: 1, m + 3: 2} if held else None,
        )
        return list(held)

    products, *grads = z_gather(err_home, functools.partial(inner, held=[]))
    dz = wid_core_sum(products)
    enc_away, enc_mine = [
        pl.pallas_call(
            functools.partial(enc_grad_kernel, NZ, o),
            out_shape=shape(row_count, half),
            in_specs=[pl.BlockSpec(memory_space=pltpu.SMEM), vm] + [far_memory] * NZ,
            out_specs=vm,
            scratch_shapes=[
                pltpu.VMEM((NZ, slots, half + 128), BF16),
                pltpu.SemaphoreType.DMA((NZ,)),
            ],
            compiler_params=pltpu.CompilerParams(vmem_limit_bytes=VMEM_LIMIT),
            cost_estimate=pl.CostEstimate(flops=8 * flops, bytes_accessed=5_000_000, transcendentals=0),
        )(ids, dz, *chosen)
        for o in (1, 0)
    ]
    dec_step, dec_m_new, dec_v_new = adam(core, grads[0], core_swap(grads[1]), dec_m, dec_v)
    enc_step, enc_m_new, enc_v_new = adam(core, enc_mine, core_swap(enc_away), enc_m, enc_v)
    return (enc_step, dec_step, enc_m_new, enc_v_new, dec_m_new, dec_v_new)


def solution(mesh):
    grid = P("lat", "wid")
    return jax.shard_map(
        local,
        mesh=mesh,
        in_specs=(grid, P("lat", None), P("wid"), grid, P("lat"), grid, grid, grid, grid, grid),
        out_specs=(grid,) * 6,
        check_vma=False,
    )
```

```python
import functools

import jax
import jax.numpy as jnp
from jax import lax
from jax.experimental import pallas as pl
from jax.experimental.pallas import tpu as pltpu
from jax.sharding import PartitionSpec as P

F32 = jnp.float32
BF16 = jnp.bfloat16
NX, NZ = 4, 8
CAP = 24
VMEM_LIMIT = 12 * 1024 * 1024
FROM = {1: (1, 3, 0, 2), -1: (2, 0, 3, 1), 2: (3, 2, 1, 0)}


def plane_shift(value, dx, dz):
    pairs = []
    for i in range(2 * NX * NZ):
        x, z, core = i // (2 * NZ), (i // 2) % NZ, i % 2
        pairs.append((i, (((x + dx) % NX) * NZ + (z + dz) % NZ) * 2 + core))
    return lax.ppermute(value, "lat", pairs)


def core_swap(value):
    return lax.ppermute(value, "lat", [(i, i ^ 1) for i in range(2 * NX * NZ)])


def tie(first, *rest):
    return lax.optimization_barrier((first, *rest))[0]


def z_gather(home, work):
    up = down = home
    half = home.shape[0] // 2
    out = [work([0], [[home]])]
    for step in range(NZ // 2):
        if step:
            up = tie(up, *jax.tree.leaves(out[-2]))
        if step < NZ // 2 - 1:
            up, down = plane_shift(up, 0, 1), plane_shift(down, 0, -1)
            out.append(work([2 * step + 1, 2 * step + 2], [[up], [down]]))
        else:
            far = [plane_shift(up[:half], 0, 1), plane_shift(down[half:], 0, -1)]
            out.append(work([NZ - 1], [far]))
    return out[-1]


def dot(a, b, dims):
    return lax.dot_general(a, b, (dims, ((), ())), preferred_element_type=F32)


def pick(dense, spread, rows_hot):
    high = dense.astype(BF16)
    low = (dense - high.astype(F32)).astype(BF16)
    by_slot = dot(high, rows_hot, ((1,), (1,))) + dot(low, rows_hot, ((1,), (1,)))
    return jnp.sum(by_slot * spread.astype(F32), axis=0, keepdims=True)


def flag(mask):
    return mask.astype(F32).astype(BF16)


def iota(dims, axis):
    return lax.broadcasted_iota(jnp.int32, dims, axis)


def hots(meta, o, tokens, row_count):
    slots = meta.shape[0] - tokens
    start = meta[:tokens, 2 * o : 2 * o + 1].astype(F32)
    end = meta[:tokens, 2 * o + 1 : 2 * o + 2].astype(F32)
    lane = iota((tokens, slots), 1).astype(F32)
    row = meta[tokens:, o : o + 1].astype(F32)
    row_one = iota((slots, row_count), 1).astype(F32) + 1.0
    return flag((lane >= start) & (lane < end)), flag(row == row_one)


def center(x, bias):
    return (x.astype(F32) - bias.astype(F32)).astype(BF16)


def joined(refs, cols=slice(None)):
    parts = [ref[:, cols] for ref in refs]
    return parts[0] if len(parts) == 1 else jnp.concatenate(parts, axis=0)


def take(refs, counts):
    refs, groups = list(refs), []
    for c in counts:
        groups.append(refs[:c])
        refs = refs[c:]
    return groups, refs


def encode_kernel(gs, counts, first, ids, *refs):
    n = len(gs)
    xs, refs = take(refs, counts)
    bias_ref, own_ref, other_ref, row_bias_ref = refs[:4]
    val_ref, metas = refs[-n - 1], refs[-n:]
    row_count, width = own_ref.shape
    tokens = sum(r.shape[0] for r in xs[0])
    slots = metas[0].shape[0] - tokens
    block = tokens * CAP // slots
    lane = iota((tokens, 128), 1)
    before = flag(iota((128, 128), 0) < iota((128, 128), 1))
    t_row, t_col = iota((tokens, tokens), 0), iota((tokens, tokens), 1)
    earlier = flag((t_col < t_row) & (t_col // block == t_row // block))
    ones = jnp.ones((128, slots), BF16)
    base = (iota((tokens, slots), 0) // block * CAP).astype(F32)
    slot_lane = iota((tokens, slots), 1).astype(F32)
    slot_one = iota((slots, 128), 0).astype(F32) + 1.0
    row_one = iota((slots, row_count), 1).astype(F32) + 1.0
    jobs = [(k, o) for k in range(n) for o in range(2)]
    infos = [joined(x, slice(width, width + 128)).astype(F32) for x in xs]
    loc_ones = [pltpu.roll(info, 96, axis=1) + 1.0 for info in infos]
    owned = [(infos[k] == ids[o].astype(F32)) & (lane < 32) for k, o in jobs]
    owned_b = [flag(w) for w in owned]
    count = [dot(w, ones, ((1,), (0,))) for w in owned_b]
    in_token = [dot(w, before, ((1,), (0,))) for w in owned_b]
    start = [base + dot(earlier, c.astype(BF16), ((1,), (0,))) for c in count]
    end = [s + c for s, c in zip(start, count)]
    spread = [flag((slot_lane >= s) & (slot_lane < e)) for s, e in zip(start, end)]
    number = [
        jnp.where(w, s[:, :128] + i + 1.0, 0.0).astype(BF16) for w, s, i in zip(owned, start, in_token)
    ]
    place = [jnp.where(w, loc_ones[k], 0.0).astype(BF16) for w, (k, o) in zip(owned, jobs)]
    slot_number = [dot(s, v, ((0,), (0,))) for s, v in zip(spread, number)]
    slot_place = [dot(s, v, ((0,), (0,))) for s, v in zip(spread, place)]
    row = [
        jnp.sum(jnp.where(v == slot_one, p, 0.0), axis=1, keepdims=True)
        for v, p in zip(slot_number, slot_place)
    ]
    centered = [center(joined(x, slice(0, width)), bias_ref[...]) for x in xs]
    for j, (k, o) in enumerate(jobs):
        rows = own_ref if o == 0 else other_ref
        dense = dot(centered[k], rows[...], ((1,), (1,)))
        if o == 0:
            dense = dense + row_bias_ref[...] * ids[2].astype(F32)
        val_ref[o, gs[k] : gs[k] + 1, :] = pick(dense, spread[j], flag(row[j] == row_one))
    slot_lane_128 = iota((slots, 128), 1)
    for k in range(n):
        s0, s1, e0, e1 = (v[2 * k + o][:, :128] for v in (start, end) for o in range(2))
        by_token = jnp.where(lane == 0, s0, jnp.where(lane == 1, e0, jnp.where(lane == 2, s1, e1)))
        metas[k][:tokens, :] = by_token.astype(BF16)
        metas[k][tokens:, :] = jnp.where(slot_lane_128 == 0, row[2 * k], row[2 * k + 1]).astype(BF16)


def select_kernel(counts, row_count, *refs):
    n = len(counts)
    xs, refs = take(refs, counts)
    metas, bias_ref, outs = refs[:n], refs[n], refs[n + 1 : 2 * n + 1]
    buffer, sems = refs[2 * n + 1 :]
    width = bias_ref.shape[1]
    copies = []
    for k in range(n):
        x = center(joined(xs[k], slice(0, width)), bias_ref[...])
        meta = metas[k][...]
        tokens = x.shape[0]
        for o in range(2):
            spread, _ = hots(meta, o, tokens, row_count)
            buffer[k, o, :, :width] = dot(spread, x, ((0,), (0,))).astype(BF16)
            buffer[k, o, :, width:] = meta[tokens:, :]
            copies.append(pltpu.make_async_copy(buffer.at[k, o], outs[k].at[o], sems.at[k, o]))
            copies[-1].start()
    for copy in copies:
        copy.wait()


def column(values):
    return jnp.transpose(jnp.broadcast_to(values, (8, values.shape[1])))[:, :1]


def recon_kernel(offsets, g, *refs):
    val_ref, meta_ref, own_ref, other_ref = refs[:4]
    come, outs = refs[4 : 4 + len(offsets)], refs[4 + len(offsets) :]
    slots = val_ref.shape[2]
    tokens = meta_ref.shape[0] - slots
    meta = meta_ref[...]
    total = None
    for o in range(2):
        spread, hot = hots(meta, o, tokens, own_ref.shape[0])
        rows = dot(hot, (own_ref if o == 0 else other_ref)[...], ((1,), (0,)))
        contrib = (column(val_ref[o, g : g + 1, :]) * rows).astype(BF16)
        term = dot(spread, contrib, ((1,), (0,)))
        total = term if total is None else total + term
    if offsets and come[0].shape[0] < tokens:
        at, part = offsets[0], come[0].shape[0]
        added = total[at : at + part] + come[0][...].astype(F32)
        total = jnp.concatenate([added, total[part:]] if at == 0 else [total[:at], added], axis=0)
    else:
        for c in come:
            total = total + c[...].astype(F32)
    if outs[0].shape[0] < tokens:
        part = outs[0].shape[0]
        for k, out in enumerate(outs):
            out[...] = total[k * part : (k + 1) * part].astype(out.dtype)
    else:
        for out in outs:
            out[...] = total.astype(out.dtype)


def err_kernel(sum_ref, up_ref, down_ref, far_up_ref, far_down_ref, x_ref, bias_ref, err_ref):
    tokens, width = err_ref.shape
    unit = tokens // NX
    piece = lambda ref, k: ref[k * unit : (k + 1) * unit, :].astype(F32)
    for k in range(NX):
        total = piece(sum_ref, k)
        total = total + piece(up_ref, FROM[1].index(k))
        total = total + piece(down_ref, FROM[-1].index(k))
        far = FROM[2].index(k)
        total = total + (piece(far_up_ref, far) if far < 2 else piece(far_down_ref, far - 2))
        recon = bias_ref[...].astype(F32) + total
        raw = x_ref[k * unit : (k + 1) * unit, :width].astype(F32)
        err_ref[k * unit : (k + 1) * unit, :] = (recon - raw).astype(BF16)


def inner_kernel(gs, counts, first, *refs):
    n = len(gs)
    errs, refs = take(refs, counts)
    metas, (pre_ref, own_ref, other_ref) = refs[:n], refs[n : n + 3]
    held, (val_ref, *grads) = refs[n + 3 : -3], refs[-3:]
    row_count = own_ref.shape[0]
    es = [joined(e) for e in errs]
    tokens = es[0].shape[0]
    for o in range(2):
        rows = own_ref if o == 0 else other_ref
        total = None
        for k, g in enumerate(gs):
            spread, hot = hots(metas[k][...], o, tokens, row_count)
            val_ref[o, g : g + 1, :] = pick(dot(es[k], rows[...], ((1,), (1,))), spread, hot)
            by_slot = dot(spread, es[k], ((0,), (0,)))
            term = (column(pre_ref[o, g : g + 1, :]) * by_slot).astype(BF16)
            grad = dot(hot, term, ((0,), (0,)))
            total = grad if total is None else total + grad
        grads[o][...] = total if first else held[1 + o][...] + total


def enc_grad_kernel(n, o, val_ref, *refs):
    sources, out, buffer, sems = refs[:n], refs[n], refs[n + 1], refs[n + 2]
    copies = [pltpu.make_async_copy(s.at[o], buffer.at[g], sems.at[g]) for g, s in enumerate(sources)]
    flight = 3
    for copy in copies[:flight]:
        copy.start()
    values = jnp.transpose(val_ref[o])
    row_count, width = out.shape
    slots = buffer.shape[1]
    row_one = iota((slots, row_count), 1).astype(F32) + 1.0
    total = None
    for g in range(n):
        copies[g].wait()
        if g + flight < n:
            copies[g + flight].start()
        term = (values[:, g : g + 1] * buffer[g, :, :width].astype(F32)).astype(BF16)
        row = buffer[g, :, width : width + 128][:, o : o + 1].astype(F32)
        grad = dot(flag(row == row_one), term, ((0,), (0,)))
        total = grad if total is None else total + grad
    out[...] = total


def adam_kernel(ids, own_ref, come_ref, m_ref, v_ref, step_ref, m_out, v_out):
    mine = pl.program_id(1) == ids[0]
    grad = jnp.where(mine, own_ref[...], come_ref[...])
    first = 0.9 * m_ref[...].astype(F32) + 0.1 * grad
    second = 0.95 * v_ref[...].astype(F32) + 0.05 * grad * grad
    scale = 1.0 / (1.0 - 0.9**10)
    step_ref[...] = first * scale / (jnp.sqrt(second * (1.0 / (1.0 - 0.95**10))) + 1e-08)
    m_out[...] = first.astype(BF16)
    v_out[...] = second.astype(BF16)


def whole(kernel, outs, args, scalars=None, flops=0, aliases=None):
    vm = pl.BlockSpec(memory_space=pltpu.VMEM)
    sm = pl.BlockSpec(memory_space=pltpu.SMEM)
    specs = ([sm] if scalars is not None else []) + [vm] * len(args)
    size = sum(a.size * a.dtype.itemsize for a in args) + sum(
        o.size * o.dtype.itemsize for o in outs
    )
    call = pl.pallas_call(
        kernel,
        out_shape=tuple(outs),
        in_specs=specs,
        out_specs=(vm,) * len(outs),
        input_output_aliases=aliases or {},
        compiler_params=pltpu.CompilerParams(vmem_limit_bytes=VMEM_LIMIT),
        cost_estimate=pl.CostEstimate(flops=flops, bytes_accessed=size, transcendentals=0),
    )
    return call(*(([scalars] if scalars is not None else []) + list(args)))


def shape(*dims, kind=F32):
    return jax.ShapeDtypeStruct(dims, kind)


def wid_core_sum(values, beside=lambda value: None):
    values = values + core_swap(values)[::-1]
    beside = beside(values)
    values = values + lax.ppermute(values, "wid", [(0, 1), (1, 0), (2, 3), (3, 2)])
    if beside is not None:
        values = tie(values, beside)
    return values + lax.ppermute(values, "wid", [(0, 3), (3, 0), (1, 2), (2, 1)])


def adam(core, own, come, moment, second):
    rows, full = moment.shape
    half = full // 2
    tile = rows // 2
    half_spec = pl.BlockSpec((tile, half), lambda i, h, ids: (i, 0))
    full_spec = pl.BlockSpec((tile, half), lambda i, h, ids: (i, h))
    return pl.pallas_call(
        adam_kernel,
        out_shape=(shape(rows, full), shape(rows, full, kind=BF16), shape(rows, full, kind=BF16)),
        grid_spec=pltpu.PrefetchScalarGridSpec(
            num_scalar_prefetch=1,
            grid=(rows // tile, 2),
            in_specs=[half_spec, half_spec, full_spec, full_spec],
            out_specs=(full_spec, full_spec, full_spec),
        ),
        compiler_params=pltpu.CompilerParams(vmem_limit_bytes=VMEM_LIMIT),
        cost_estimate=pl.CostEstimate(
            flops=rows * full * 12, bytes_accessed=rows * full * 16, transcendentals=0
        ),
    )(core.reshape(1), own, come, moment, second)


def local(tokens, latent_rows, dec_bias, enc_rows, latent_encoder_bias, dec_rows, enc_m, enc_v, dec_m, dec_v):
    me = lax.axis_index("lat")
    core = me % 2
    tok_dev, full = tokens.shape
    row_count = enc_rows.shape[0]
    half = full // 2
    mine, other = core * half, (1 - core) * half
    first_wid = (lax.axis_index("wid") == 0).astype(jnp.int32)
    ids = jnp.stack([me, me ^ 1, first_wid]).astype(jnp.int32)

    info = jnp.concatenate(
        [
            (latent_rows // row_count).astype(BF16),
            (latent_rows % row_count).astype(BF16),
            jnp.zeros((tok_dev, 128 - 2 * latent_rows.shape[1]), BF16),
        ],
        axis=1,
    )
    cut = lambda a, at: lax.dynamic_slice_in_dim(a, at, half, axis=a.ndim - 1)
    own_part = jnp.concatenate([cut(tokens, mine), info], axis=1)
    come_part = core_swap(jnp.concatenate([cut(tokens, other), info], axis=1))
    even = core == 0
    unit = jnp.concatenate(
        [jnp.where(even, own_part, come_part), jnp.where(even, come_part, own_part)], axis=0
    )
    near = [unit] + [plane_shift(unit, dx, 0) for dx in (1, -1, 2)]
    enc_rows, dec_rows = lax.optimization_barrier((enc_rows, dec_rows, unit))[:2]
    bias_half = cut(dec_bias, mine).reshape(1, half)
    row_bias = latent_encoder_bias.reshape(1, row_count)
    enc_own, dec_own = cut(enc_rows, mine), cut(dec_rows, mine)
    enc_other, dec_other = core_swap(cut(enc_rows, other)), core_swap(cut(dec_rows, other))
    home = tie(jnp.concatenate(near, axis=0), enc_own, enc_other, dec_own, dec_other)

    group_tok = home.shape[0]
    slots = group_tok // tok_dev * CAP
    flops = 2 * group_tok * 2 * row_count * half
    xs, metas = {}, {}
    vals_shape = shape(2, NZ, slots)

    def encode(gs, groups, held=[]):
        n = len(gs)
        args = [part for x in groups for part in x] + [bias_half, enc_own, enc_other, row_bias]
        held[:], found = (
            lambda out: (out[:1], out[1:])
        )(
            whole(
                functools.partial(encode_kernel, gs, [len(x) for x in groups], not held),
                [vals_shape] + [shape(group_tok + slots, 128, kind=BF16)] * n,
                args + held,
                scalars=ids,
                flops=3 * flops * n,
                aliases={len(args) + 1: 0} if held else None,
            )
        )
        for k, g in enumerate(gs):
            xs[g], metas[g] = groups[k], found[k]
        return list(held)

    pre = wid_core_sum(z_gather(home, functools.partial(encode, held=[]))[0])

    def recon(g, come=(), offsets=(), kinds=(BF16,), rows=group_tok):
        return whole(
            functools.partial(recon_kernel, offsets or (0,) * len(come), g),
            [shape(rows, half, kind=k) for k in kinds],
            [pre, metas[g], dec_own, dec_other] + list(come),
            flops=2 * flops,
        )

    vm, far_memory = pl.BlockSpec(memory_space=pltpu.VMEM), pl.BlockSpec(memory_space=pltpu.HBM)

    def select(gs, after):
        args = [part for g in gs for part in xs[g]] + [tie(metas[g], after) for g in gs] + [bias_half]
        out = shape(2, slots, half + 128, kind=BF16)
        return pl.pallas_call(
            functools.partial(select_kernel, [len(xs[g]) for g in gs], row_count),
            out_shape=(out,) * len(gs),
            in_specs=[vm] * len(args),
            out_specs=(far_memory,) * len(gs),
            scratch_shapes=[
                pltpu.VMEM((len(gs),) + out.shape, BF16),
                pltpu.SemaphoreType.DMA((len(gs), 2)),
            ],
            compiler_params=pltpu.CompilerParams(vmem_limit_bytes=VMEM_LIMIT),
            cost_estimate=pl.CostEstimate(flops=2 * flops, bytes_accessed=2_500_000, transcendentals=0),
        )(*args)

    half_rows = group_tok // 2
    up, down = recon(NZ - 1, kinds=(BF16, BF16), rows=half_rows)
    chosen = []
    for step in range(1, NZ // 2):
        picked = select([2 * step - 2, 2 * step - 1], up)
        offsets = ((0,), (half_rows,)) if step == 1 else ((0,), (0,))
        come_up, come_down = plane_shift(up, 0, -1), plane_shift(down, 0, 1)
        (up,) = recon(NZ - 1 - 2 * step, [come_up], offsets[0])
        (down,) = recon(NZ - 2 * step, [come_down], offsets[1])
        chosen += picked
        up = tie(up, *picked)
    last = select([NZ - 2, NZ - 1], up)
    chosen += last
    come = [plane_shift(up, 0, -1), plane_shift(down, 0, 1)]
    exact, sent = recon(0, come, kinds=(F32, BF16))
    sent = tie(sent, *last)
    right, left = plane_shift(sent, 1, 0), plane_shift(sent, -1, 0)
    far_right, far_left = plane_shift(right[:half_rows], 1, 0), plane_shift(left[half_rows:], -1, 0)
    (err_home,) = whole(
        err_kernel,
        [shape(group_tok, half, kind=BF16)],
        [exact, right, left, far_right, far_left, home, bias_half],
    )

    def inner(gs, groups, held):
        args = [part for e in groups for part in e] + [metas[g] for g in gs] + [pre, dec_own, dec_other]
        m = len(args)
        held[:] = whole(
            functools.partial(inner_kernel, gs, [len(e) for e in groups], not held),
            [vals_shape] + [shape(row_count, half)] * 2,
            args + held,
            flops=4 * flops * len(gs),
            aliases={m: 0, m + 1: 1, m + 2: 2} if held else None,
        )
        return list(held)

    products, *grads = z_gather(err_home, functools.partial(inner, held=[]))
    dec_new = []

    def dec_update(started):
        dec_new[:] = adam(core, grads[0], core_swap(tie(grads[1], started)), dec_m, dec_v)
        return dec_new[1]

    dz = wid_core_sum(products, dec_update)
    dec_step, dec_m_new, dec_v_new = dec_new
    enc_away, enc_mine = [
        pl.pallas_call(
            functools.partial(enc_grad_kernel, NZ, o),
            out_shape=shape(row_count, half),
            in_specs=[vm] + [far_memory] * NZ,
            out_specs=vm,
            scratch_shapes=[
                pltpu.VMEM((NZ, slots, half + 128), BF16),
                pltpu.SemaphoreType.DMA((NZ,)),
            ],
            compiler_params=pltpu.CompilerParams(vmem_limit_bytes=VMEM_LIMIT),
            cost_estimate=pl.CostEstimate(flops=8 * flops, bytes_accessed=5_000_000, transcendentals=0),
        )(dz, *chosen)
        for o in (1, 0)
    ]
    enc_step, enc_m_new, enc_v_new = adam(core, enc_mine, core_swap(enc_away), enc_m, enc_v)
    return (enc_step, dec_step, enc_m_new, enc_v_new, dec_m_new, dec_v_new)


def solution(mesh):
    grid = P("lat", "wid")
    return jax.shard_map(
        local,
        mesh=mesh,
        in_specs=(grid, P("lat", None), P("wid"), grid, P("lat"), grid, grid, grid, grid, grid),
        out_specs=(grid,) * 6,
        check_vma=False,
    )
```

```python
import functools

import jax
import jax.numpy as jnp
from jax import lax
from jax.experimental import pallas as pl
from jax.experimental.pallas import tpu as pltpu
from jax.sharding import PartitionSpec as P

F32 = jnp.float32
BF16 = jnp.bfloat16
NX, NZ = 4, 8
CAP = 24
VMEM_LIMIT = 12 * 1024 * 1024
FROM = {1: (1, 3, 0, 2), -1: (2, 0, 3, 1), 2: (3, 2, 1, 0)}


def plane_shift(value, dx, dz):
    pairs = []
    for i in range(2 * NX * NZ):
        x, z, core = i // (2 * NZ), (i // 2) % NZ, i % 2
        pairs.append((i, (((x + dx) % NX) * NZ + (z + dz) % NZ) * 2 + core))
    return lax.ppermute(value, "lat", pairs)


def core_swap(value):
    return lax.ppermute(value, "lat", [(i, i ^ 1) for i in range(2 * NX * NZ)])


def tie(first, *rest):
    return lax.optimization_barrier((first, *rest))[0]


def z_gather(home, work):
    up = down = home
    half = home.shape[0] // 2
    out = [work([0], [[home]])]
    for step in range(NZ // 2):
        if step:
            up = tie(up, *jax.tree.leaves(out[-2]))
        if step < NZ // 2 - 1:
            up, down = plane_shift(up, 0, 1), plane_shift(down, 0, -1)
            out.append(work([2 * step + 1, 2 * step + 2], [[up], [down]]))
        else:
            far = [plane_shift(up[:half], 0, 1), plane_shift(down[half:], 0, -1)]
            out.append(work([NZ - 1], [far]))
    return out[-1]


def dot(a, b, dims):
    return lax.dot_general(a, b, (dims, ((), ())), preferred_element_type=F32)


def pick(dense, spread, rows_hot):
    high = dense.astype(BF16)
    low = (dense - high.astype(F32)).astype(BF16)
    by_slot = dot(high, rows_hot, ((1,), (1,))) + dot(low, rows_hot, ((1,), (1,)))
    return jnp.sum(by_slot * spread.astype(F32), axis=0, keepdims=True)


def flag(mask):
    return mask.astype(F32).astype(BF16)


def iota(dims, axis):
    return lax.broadcasted_iota(jnp.int32, dims, axis)


def hots(meta, o, tokens, row_count):
    slots = meta.shape[0] - tokens
    start = meta[:tokens, 2 * o : 2 * o + 1].astype(F32)
    end = meta[:tokens, 2 * o + 1 : 2 * o + 2].astype(F32)
    lane = iota((tokens, slots), 1).astype(F32)
    row = meta[tokens:, o : o + 1].astype(F32)
    row_one = iota((slots, row_count), 1).astype(F32) + 1.0
    return flag((lane >= start) & (lane < end)), flag(row == row_one)


def center(x, bias):
    return (x.astype(F32) - bias.astype(F32)).astype(BF16)


def joined(refs, cols=slice(None)):
    parts = [ref[:, cols] for ref in refs]
    return parts[0] if len(parts) == 1 else jnp.concatenate(parts, axis=0)


def take(refs, counts):
    refs, groups = list(refs), []
    for c in counts:
        groups.append(refs[:c])
        refs = refs[c:]
    return groups, refs


def encode_kernel(gs, counts, first, ids, *refs):
    n = len(gs)
    xs, refs = take(refs, counts)
    bias_ref, own_ref, other_ref, row_bias_ref = refs[:4]
    val_ref, metas = refs[-n - 1], refs[-n:]
    row_count, width = own_ref.shape
    tokens = sum(r.shape[0] for r in xs[0])
    slots = metas[0].shape[0] - tokens
    block = tokens * CAP // slots
    lane = iota((tokens, 128), 1)
    before = flag(iota((128, 128), 0) < iota((128, 128), 1))
    t_row, t_col = iota((tokens, tokens), 0), iota((tokens, tokens), 1)
    earlier = flag((t_col < t_row) & (t_col // block == t_row // block))
    ones = jnp.ones((128, slots), BF16)
    base = (iota((tokens, slots), 0) // block * CAP).astype(F32)
    slot_lane = iota((tokens, slots), 1).astype(F32)
    slot_one = iota((slots, 128), 0).astype(F32) + 1.0
    row_one = iota((slots, row_count), 1).astype(F32) + 1.0
    jobs = [(k, o) for k in range(n) for o in range(2)]
    infos = [joined(x, slice(width, width + 128)).astype(F32) for x in xs]
    loc_ones = [pltpu.roll(info, 96, axis=1) + 1.0 for info in infos]
    owned = [(infos[k] == ids[o].astype(F32)) & (lane < 32) for k, o in jobs]
    owned_b = [flag(w) for w in owned]
    count = [dot(w, ones, ((1,), (0,))) for w in owned_b]
    in_token = [dot(w, before, ((1,), (0,))) for w in owned_b]
    start = [base + dot(earlier, c.astype(BF16), ((1,), (0,))) for c in count]
    end = [s + c for s, c in zip(start, count)]
    spread = [flag((slot_lane >= s) & (slot_lane < e)) for s, e in zip(start, end)]
    number = [
        jnp.where(w, s[:, :128] + i + 1.0, 0.0).astype(BF16) for w, s, i in zip(owned, start, in_token)
    ]
    place = [jnp.where(w, loc_ones[k], 0.0).astype(BF16) for w, (k, o) in zip(owned, jobs)]
    slot_number = [dot(s, v, ((0,), (0,))) for s, v in zip(spread, number)]
    slot_place = [dot(s, v, ((0,), (0,))) for s, v in zip(spread, place)]
    row = [
        jnp.sum(jnp.where(v == slot_one, p, 0.0), axis=1, keepdims=True)
        for v, p in zip(slot_number, slot_place)
    ]
    centered = [center(joined(x, slice(0, width)), bias_ref[...]) for x in xs]
    for j, (k, o) in enumerate(jobs):
        rows = own_ref if o == 0 else other_ref
        dense = dot(centered[k], rows[...], ((1,), (1,)))
        if o == 0:
            dense = dense + row_bias_ref[...] * ids[2].astype(F32)
        val_ref[o, gs[k] : gs[k] + 1, :] = pick(dense, spread[j], flag(row[j] == row_one))
    slot_lane_128 = iota((slots, 128), 1)
    for k in range(n):
        s0, s1, e0, e1 = (v[2 * k + o][:, :128] for v in (start, end) for o in range(2))
        by_token = jnp.where(lane == 0, s0, jnp.where(lane == 1, e0, jnp.where(lane == 2, s1, e1)))
        metas[k][:tokens, :] = by_token.astype(BF16)
        metas[k][tokens:, :] = jnp.where(slot_lane_128 == 0, row[2 * k], row[2 * k + 1]).astype(BF16)


def select_kernel(counts, row_count, *refs):
    n = len(counts)
    xs, refs = take(refs, counts)
    metas, bias_ref, outs = refs[:n], refs[n], refs[n + 1 : 2 * n + 1]
    buffer, sems = refs[2 * n + 1 :]
    width = bias_ref.shape[1]
    copies = []
    for k in range(n):
        x = center(joined(xs[k], slice(0, width)), bias_ref[...])
        meta = metas[k][...]
        tokens = x.shape[0]
        for o in range(2):
            spread, _ = hots(meta, o, tokens, row_count)
            buffer[k, o, :, :width] = dot(spread, x, ((0,), (0,))).astype(BF16)
            buffer[k, o, :, width:] = meta[tokens:, :]
            copies.append(pltpu.make_async_copy(buffer.at[k, o], outs[k].at[o], sems.at[k, o]))
            copies[-1].start()
    for copy in copies:
        copy.wait()


def column(values):
    return jnp.transpose(jnp.broadcast_to(values, (8, values.shape[1])))[:, :1]


def recon_kernel(offsets, g, *refs):
    val_ref, meta_ref, own_ref, other_ref = refs[:4]
    come, outs = refs[4 : 4 + len(offsets)], refs[4 + len(offsets) :]
    slots = val_ref.shape[2]
    tokens = meta_ref.shape[0] - slots
    meta = meta_ref[...]
    total = None
    for o in range(2):
        spread, hot = hots(meta, o, tokens, own_ref.shape[0])
        rows = dot(hot, (own_ref if o == 0 else other_ref)[...], ((1,), (0,)))
        contrib = (column(val_ref[o, g : g + 1, :]) * rows).astype(BF16)
        term = dot(spread, contrib, ((1,), (0,)))
        total = term if total is None else total + term
    if offsets and come[0].shape[0] < tokens:
        at, part = offsets[0], come[0].shape[0]
        added = total[at : at + part] + come[0][...].astype(F32)
        total = jnp.concatenate([added, total[part:]] if at == 0 else [total[:at], added], axis=0)
    else:
        for c in come:
            total = total + c[...].astype(F32)
    if outs[0].shape[0] < tokens:
        part = outs[0].shape[0]
        for k, out in enumerate(outs):
            out[...] = total[k * part : (k + 1) * part].astype(out.dtype)
    else:
        for out in outs:
            out[...] = total.astype(out.dtype)


def err_kernel(sum_ref, up_ref, down_ref, far_up_ref, far_down_ref, x_ref, bias_ref, err_ref):
    tokens, width = err_ref.shape
    unit = tokens // NX
    piece = lambda ref, k: ref[k * unit : (k + 1) * unit, :].astype(F32)
    for k in range(NX):
        total = piece(sum_ref, k)
        total = total + piece(up_ref, FROM[1].index(k))
        total = total + piece(down_ref, FROM[-1].index(k))
        far = FROM[2].index(k)
        total = total + (piece(far_up_ref, far) if far < 2 else piece(far_down_ref, far - 2))
        recon = bias_ref[...].astype(F32) + total
        raw = x_ref[k * unit : (k + 1) * unit, :width].astype(F32)
        err_ref[k * unit : (k + 1) * unit, :] = (recon - raw).astype(BF16)


def inner_kernel(gs, counts, first, *refs):
    n = len(gs)
    errs, refs = take(refs, counts)
    metas, (pre_ref, own_ref, other_ref) = refs[:n], refs[n : n + 3]
    held, (val_ref, *grads) = refs[n + 3 : -3], refs[-3:]
    row_count = own_ref.shape[0]
    es = [joined(e) for e in errs]
    tokens = es[0].shape[0]
    for o in range(2):
        rows = own_ref if o == 0 else other_ref
        total = None
        for k, g in enumerate(gs):
            spread, hot = hots(metas[k][...], o, tokens, row_count)
            val_ref[o, g : g + 1, :] = pick(dot(es[k], rows[...], ((1,), (1,))), spread, hot)
            by_slot = dot(spread, es[k], ((0,), (0,)))
            term = (column(pre_ref[o, g : g + 1, :]) * by_slot).astype(BF16)
            grad = dot(hot, term, ((0,), (0,)))
            total = grad if total is None else total + grad
        grads[o][...] = total if first else held[1 + o][...] + total


def enc_grad_kernel(n, val_ref, *refs):
    sources, outs, buffer, sems = refs[:n], refs[n : n + 2], refs[n + 2], refs[n + 3]
    row_count, width = outs[0].shape
    slots = buffer.shape[2]
    row_one = iota((slots, row_count), 1).astype(F32) + 1.0
    copies = {
        (o, g): pltpu.make_async_copy(sources[g].at[o], buffer.at[o, g], sems.at[o, g])
        for o in (1, 0)
        for g in range(n)
    }
    for copy in copies.values():
        copy.start()
    for o in (1, 0):
        values = jnp.transpose(val_ref[o])
        for g in range(n):
            copies[o, g].wait()
        total = None
        for g in range(n):
            term = (values[:, g : g + 1] * buffer[o, g, :, :width].astype(F32)).astype(BF16)
            row = buffer[o, g, :, width : width + 128][:, o : o + 1].astype(F32)
            grad = dot(flag(row == row_one), term, ((0,), (0,)))
            total = grad if total is None else total + grad
        outs[o][...] = total


def adam_kernel(ids, own_ref, come_ref, m_ref, v_ref, step_ref, m_out, v_out):
    mine = pl.program_id(1) == ids[0]
    grad = jnp.where(mine, own_ref[...], come_ref[...])
    first = 0.9 * m_ref[...].astype(F32) + 0.1 * grad
    second = 0.95 * v_ref[...].astype(F32) + 0.05 * grad * grad
    scale = 1.0 / (1.0 - 0.9**10)
    step_ref[...] = first * scale / (jnp.sqrt(second * (1.0 / (1.0 - 0.95**10))) + 1e-08)
    m_out[...] = first.astype(BF16)
    v_out[...] = second.astype(BF16)


def whole(kernel, outs, args, scalars=None, flops=0, aliases=None):
    vm = pl.BlockSpec(memory_space=pltpu.VMEM)
    sm = pl.BlockSpec(memory_space=pltpu.SMEM)
    specs = ([sm] if scalars is not None else []) + [vm] * len(args)
    size = sum(a.size * a.dtype.itemsize for a in args) + sum(
        o.size * o.dtype.itemsize for o in outs
    )
    call = pl.pallas_call(
        kernel,
        out_shape=tuple(outs),
        in_specs=specs,
        out_specs=(vm,) * len(outs),
        input_output_aliases=aliases or {},
        compiler_params=pltpu.CompilerParams(vmem_limit_bytes=VMEM_LIMIT),
        cost_estimate=pl.CostEstimate(flops=flops, bytes_accessed=size, transcendentals=0),
    )
    return call(*(([scalars] if scalars is not None else []) + list(args)))


def shape(*dims, kind=F32):
    return jax.ShapeDtypeStruct(dims, kind)


def wid_core_sum(values):
    values = values + core_swap(values)[::-1]
    for pairs in ([(0, 1), (1, 0), (2, 3), (3, 2)], [(0, 2), (2, 0), (1, 3), (3, 1)]):
        values = values + lax.ppermute(values, "wid", pairs)
    return values


def adam(core, own, come, moment, second):
    rows, full = moment.shape
    half = full // 2
    tile = rows // 2
    half_spec = pl.BlockSpec((tile, half), lambda i, h, ids: (i, 0))
    full_spec = pl.BlockSpec((tile, half), lambda i, h, ids: (i, h))
    return pl.pallas_call(
        adam_kernel,
        out_shape=(shape(rows, full), shape(rows, full, kind=BF16), shape(rows, full, kind=BF16)),
        grid_spec=pltpu.PrefetchScalarGridSpec(
            num_scalar_prefetch=1,
            grid=(rows // tile, 2),
            in_specs=[half_spec, half_spec, full_spec, full_spec],
            out_specs=(full_spec, full_spec, full_spec),
        ),
        compiler_params=pltpu.CompilerParams(vmem_limit_bytes=VMEM_LIMIT),
        cost_estimate=pl.CostEstimate(
            flops=rows * full * 12, bytes_accessed=rows * full * 16, transcendentals=0
        ),
    )(core.reshape(1), own, come, moment, second)


def local(tokens, latent_rows, dec_bias, enc_rows, latent_encoder_bias, dec_rows, enc_m, enc_v, dec_m, dec_v):
    me = lax.axis_index("lat")
    core = me % 2
    tok_dev, full = tokens.shape
    row_count = enc_rows.shape[0]
    half = full // 2
    mine, other = core * half, (1 - core) * half
    first_wid = (lax.axis_index("wid") == 0).astype(jnp.int32)
    ids = jnp.stack([me, me ^ 1, first_wid]).astype(jnp.int32)

    info = jnp.concatenate(
        [
            (latent_rows // row_count).astype(BF16),
            (latent_rows % row_count).astype(BF16),
            jnp.zeros((tok_dev, 128 - 2 * latent_rows.shape[1]), BF16),
        ],
        axis=1,
    )
    cut = lambda a, at: lax.dynamic_slice_in_dim(a, at, half, axis=a.ndim - 1)
    own_part = jnp.concatenate([cut(tokens, mine), info], axis=1)
    come_part = core_swap(jnp.concatenate([cut(tokens, other), info], axis=1))
    even = core == 0
    unit = jnp.concatenate(
        [jnp.where(even, own_part, come_part), jnp.where(even, come_part, own_part)], axis=0
    )
    near = [unit] + [plane_shift(unit, dx, 0) for dx in (1, -1, 2)]
    enc_rows, dec_rows = lax.optimization_barrier((enc_rows, dec_rows, unit))[:2]
    bias_half = cut(dec_bias, mine).reshape(1, half)
    row_bias = latent_encoder_bias.reshape(1, row_count)
    enc_own, dec_own = cut(enc_rows, mine), cut(dec_rows, mine)
    enc_other, dec_other = core_swap(cut(enc_rows, other)), core_swap(cut(dec_rows, other))
    home = tie(jnp.concatenate(near, axis=0), enc_own, enc_other, dec_own, dec_other)

    group_tok = home.shape[0]
    slots = group_tok // tok_dev * CAP
    flops = 2 * group_tok * 2 * row_count * half
    xs, metas = {}, {}
    vals_shape = shape(2, NZ, slots)

    def encode(gs, groups, held=[]):
        n = len(gs)
        args = [part for x in groups for part in x] + [bias_half, enc_own, enc_other, row_bias]
        held[:], found = (
            lambda out: (out[:1], out[1:])
        )(
            whole(
                functools.partial(encode_kernel, gs, [len(x) for x in groups], not held),
                [vals_shape] + [shape(group_tok + slots, 128, kind=BF16)] * n,
                args + held,
                scalars=ids,
                flops=3 * flops * n,
                aliases={len(args) + 1: 0} if held else None,
            )
        )
        for k, g in enumerate(gs):
            xs[g], metas[g] = groups[k], found[k]
        return list(held)

    pre = wid_core_sum(z_gather(home, functools.partial(encode, held=[]))[0])

    def recon(g, come=(), offsets=(), kinds=(BF16,), rows=group_tok):
        return whole(
            functools.partial(recon_kernel, offsets or (0,) * len(come), g),
            [shape(rows, half, kind=k) for k in kinds],
            [pre, metas[g], dec_own, dec_other] + list(come),
            flops=2 * flops,
        )

    vm, far_memory = pl.BlockSpec(memory_space=pltpu.VMEM), pl.BlockSpec(memory_space=pltpu.HBM)

    def select(gs, after):
        args = [part for g in gs for part in xs[g]] + [tie(metas[g], after) for g in gs] + [bias_half]
        out = shape(2, slots, half + 128, kind=BF16)
        return pl.pallas_call(
            functools.partial(select_kernel, [len(xs[g]) for g in gs], row_count),
            out_shape=(out,) * len(gs),
            in_specs=[vm] * len(args),
            out_specs=(far_memory,) * len(gs),
            scratch_shapes=[
                pltpu.VMEM((len(gs),) + out.shape, BF16),
                pltpu.SemaphoreType.DMA((len(gs), 2)),
            ],
            compiler_params=pltpu.CompilerParams(vmem_limit_bytes=VMEM_LIMIT),
            cost_estimate=pl.CostEstimate(flops=2 * flops, bytes_accessed=2_500_000, transcendentals=0),
        )(*args)

    half_rows = group_tok // 2
    up, down = recon(NZ - 1, kinds=(BF16, BF16), rows=half_rows)
    chosen = []
    for step in range(1, NZ // 2):
        picked = select([2 * step - 4, 2 * step - 3], up) if step > 1 else ()
        offsets = ((0,), (half_rows,)) if step == 1 else ((0,), (0,))
        come_up, come_down = plane_shift(up, 0, -1), plane_shift(down, 0, 1)
        (up,) = recon(NZ - 1 - 2 * step, [come_up], offsets[0])
        (down,) = recon(NZ - 2 * step, [come_down], offsets[1])
        chosen += picked
        if picked:
            up = tie(up, *picked)
    picked = select([NZ - 4, NZ - 3], up)
    come = [plane_shift(up, 0, -1), plane_shift(down, 0, 1)]
    exact, sent = recon(0, come, kinds=(F32, BF16))
    sent = tie(sent, *picked)
    last = select([NZ - 2, NZ - 1], sent)
    chosen += [*picked, *last]
    right, left = plane_shift(sent, 1, 0), plane_shift(sent, -1, 0)
    far_right = plane_shift(tie(right, *last)[:half_rows], 1, 0)
    far_left = plane_shift(left[half_rows:], -1, 0)
    (err_home,) = whole(
        err_kernel,
        [shape(group_tok, half, kind=BF16)],
        [exact, right, left, far_right, far_left, home, bias_half],
    )

    def inner(gs, groups, held):
        args = [part for e in groups for part in e] + [metas[g] for g in gs] + [pre, dec_own, dec_other]
        m = len(args)
        held[:] = whole(
            functools.partial(inner_kernel, gs, [len(e) for e in groups], not held),
            [vals_shape] + [shape(row_count, half)] * 2,
            args + held,
            flops=4 * flops * len(gs),
            aliases={m: 0, m + 1: 1, m + 2: 2} if held else None,
        )
        return list(held)

    products, *grads = z_gather(err_home, functools.partial(inner, held=[]))
    dz = wid_core_sum(products)
    enc_mine, enc_away = pl.pallas_call(
        functools.partial(enc_grad_kernel, NZ),
        out_shape=(shape(row_count, half),) * 2,
        in_specs=[vm] + [far_memory] * NZ,
        out_specs=(vm, vm),
        scratch_shapes=[
            pltpu.VMEM((2, NZ, slots, half + 128), BF16),
            pltpu.SemaphoreType.DMA((2, NZ)),
        ],
        compiler_params=pltpu.CompilerParams(vmem_limit_bytes=VMEM_LIMIT),
        cost_estimate=pl.CostEstimate(flops=16 * flops, bytes_accessed=10_000_000, transcendentals=0),
    )(dz, *chosen)
    dec_step, dec_m_new, dec_v_new = adam(core, grads[0], core_swap(grads[1]), dec_m, dec_v)
    enc_step, enc_m_new, enc_v_new = adam(core, enc_mine, core_swap(enc_away), enc_m, enc_v)
    return (enc_step, dec_step, enc_m_new, enc_v_new, dec_m_new, dec_v_new)


def solution(mesh):
    grid = P("lat", "wid")
    return jax.shard_map(
        local,
        mesh=mesh,
        in_specs=(grid, P("lat", None), P("wid"), grid, P("lat"), grid, grid, grid, grid, grid),
        out_specs=(grid,) * 6,
        check_vma=False,
    )
```
